128 devices in a mesh: row: 2 (over core), col: 4 (over x), depth: 16 (over z, y).
Axes of the slice: x: 4, y: 4, z: 4, core: 2. Of those that a mesh axis runs over, the one named last changes fastest.
Arguments:
- tokens: bfloat16 [3072, 4096], P(('col', 'depth'), 'row'), may hold values from -6 to 6
- gate_weight: bfloat16 [4096, 14336], P('row', 'col'), may hold values from -0.09375 to 0.09375
- up_weight: bfloat16 [4096, 14336], P('row', 'col'), may hold values from -0.09375 to 0.09375
- down_weight: bfloat16 [14336, 4096], P('col', 'row'), may hold values from -0.046875 to 0.046875
- cotangent: bfloat16 [3072, 4096], P(('col', 'depth'), 'row'), may hold values from -16 to 16
Outputs:
- mixed: bfloat16 [3072, 4096], P(('col', 'depth'), 'row')
- input_grad: bfloat16 [3072, 4096], P(('col', 'depth'), 'row')
- gate_grad: bfloat16 [4096, 14336], P('row', ('col', 'depth'))
- up_grad: bfloat16 [4096, 14336], P('row', ('col', 'depth'))
- down_grad: bfloat16 [14336, 4096], P('col', ('row', 'depth'))
The draws below stay inside these ranges and needn't reach their ends.
All inputs are finite; a program needn't handle non-finite values.
Results may differ from the reference program's by a relative error of at most 0.027.
Values may be sent and summed in bfloat16 or wider, within the bound.
No kernel may reach another device: no remote copies, remote signals or barrier semaphores. Data moves between devices by JAX's collectives and lax.ppermute only.
A program may use at most 192 MiB of HBM per device.

```python
import jax
import jax.numpy as jnp

D = 4096
FF = 14336
TOK_DEV = 48
TOKENS = 3072
N_COL = 4
N_DEPTH = 16


def strengthened(drawn, key, source, target, shards_of, factor):
    def block_of(dim):
        return (jnp.arange(drawn.shape[dim]) // (drawn.shape[dim] // shards_of)).reshape((-1,) + (1,) * (drawn.ndim - 1 - dim))

    near = jax.random.permutation(key, shards_of)[block_of(target)]
    other_side = (block_of(target) + shards_of // 2) % shards_of
    return jnp.where((block_of(source) == near) | (block_of(source) == other_side), factor * drawn, drawn)


def level_of(own_key, extent, cuts, smallest, top_value):
    def one(position, shards_of):
        heights = jax.random.uniform(jax.random.fold_in(jax.random.fold_in(own_key, 6), position), (shards_of,), jnp.float32, smallest / len(cuts), top_value / len(cuts))
        return jnp.repeat(jnp.exp(heights), extent[position] // shards_of).reshape((-1,) + (1,) * (len(extent) - position - 1))

    loudness = one(*cuts[0])
    for cut in cuts[1:]:
        loudness = loudness * one(*cut)
    return loudness


def noise(rng, shape, width, reach, shards=(), kind=jnp.bfloat16):
    result = width * jax.random.normal(rng, shape, jnp.float32)
    if shards:
        result = result * level_of(rng, shape, shards, -0.22, 0.18)
    return jnp.clip(result, -reach, reach).astype(kind)


def heavy_noise(rng, dims, scale, limit, split, heavy, held_as=jnp.bfloat16):
    values = scale * jax.random.normal(rng, dims, jnp.float32)
    if split:
        values = values * level_of(rng, dims, split, -0.22, 0.18)
    return jnp.clip(strengthened(values, jax.random.fold_in(rng, 3), *heavy), -limit, limit).astype(held_as)


def setup_inputs(seed: int = 0) -> dict:
    splits = jax.random.split(jax.random.key(seed), 6)
    tokens = noise(splits[0], (TOKENS, D), 1.0, 6.0, ((0, 64), (1, 2)))
    gate_weight = noise(splits[1], (D, FF), D ** -0.5, 0.09375, ((0, 2), (1, 4)))
    up_weight = noise(splits[2], (D, FF), D ** -0.5, 0.09375, ((0, 2), (1, 4)))
    down_weight = noise(splits[3], (FF, D), FF ** -0.5, 0.046875, ((0, 4), (1, 2)))
    cotangent = heavy_noise(splits[4], (TOKENS, D), 1.0, 16.0, ((0, 64), (1, 2)), (0, 1, 64, 4.0))
    return {"tokens": tokens, "gate_weight": gate_weight, "up_weight": up_weight, "down_weight": down_weight, "cotangent": cotangent}


def swiglu_grads(gate_vals, up_vals, hidden_grad):
    sigmoid_part = jax.nn.sigmoid(gate_vals)
    grad_up = (hidden_grad * gate_vals * sigmoid_part).astype(jnp.bfloat16)
    grad_gate = (hidden_grad * up_vals * sigmoid_part * (1.0 + gate_vals * (1.0 - sigmoid_part))).astype(jnp.bfloat16)
    return grad_gate, grad_up


def by_slice(array, slice_index):
    shaped = array.reshape(N_COL, N_DEPTH, TOK_DEV, array.shape[1])
    return shaped[:, slice_index].reshape(N_COL * TOK_DEV, array.shape[1])


def rounded_partial(left, right):
    product = jnp.dot(left.T, right, preferred_element_type=jnp.float32).astype(jnp.bfloat16)
    return product.astype(jnp.float32)


def reference(tokens, gate_weight, up_weight, down_weight, cotangent):
    gate_vals = jnp.dot(tokens, gate_weight, preferred_element_type=jnp.float32)
    up_vals = jnp.dot(tokens, up_weight, preferred_element_type=jnp.float32)
    hidden = (jax.nn.silu(gate_vals) * up_vals).astype(jnp.bfloat16)
    mixed = jnp.dot(hidden, down_weight, preferred_element_type=jnp.float32).astype(jnp.bfloat16)
    hidden_grad = jnp.dot(cotangent, down_weight.T, preferred_element_type=jnp.float32)
    grad_gate, grad_up = swiglu_grads(gate_vals, up_vals, hidden_grad)
    input_grad = (jnp.dot(grad_gate, gate_weight.T, preferred_element_type=jnp.float32)
                  + jnp.dot(grad_up, up_weight.T, preferred_element_type=jnp.float32)).astype(jnp.bfloat16)
    gate_total = jnp.zeros((D, FF), jnp.float32)
    up_total = jnp.zeros((D, FF), jnp.float32)
    down_total = jnp.zeros((FF, D), jnp.float32)
    for slice_index in range(N_DEPTH):
        slice_tokens = by_slice(tokens, slice_index)
        gate_total = gate_total + rounded_partial(slice_tokens, by_slice(grad_gate, slice_index))
        up_total = up_total + rounded_partial(slice_tokens, by_slice(grad_up, slice_index))
        down_total = down_total + rounded_partial(by_slice(hidden, slice_index), by_slice(cotangent, slice_index))
    return (mixed, input_grad, gate_total.astype(jnp.bfloat16), up_total.astype(jnp.bfloat16),
            down_total.astype(jnp.bfloat16))
```

```python
import jax
import jax.numpy as jnp
from jax import lax
from jax.experimental import pallas as pl
from jax.experimental.pallas import tpu as pltpu
from jax.sharding import PartitionSpec as P

N_COL = 4
N_DEPTH = 16
SIDE = 4
BF16 = jnp.bfloat16
F32 = jnp.float32


def shifted(axis, index, step):
    if axis == "x":
        return (index + step) % N_COL
    z, y = divmod(index, SIDE)
    if axis == "y":
        return z * SIDE + (y + step) % SIDE
    return ((z + step) % SIDE) * SIDE + y


def extent(axis):
    return N_COL if axis == "x" else N_DEPTH


def mesh_axis(axis):
    return "col" if axis == "x" else "depth"


def hop(array, axis):
    n = extent(axis)
    pairs = [
        (core * n + i, core * n + shifted(axis, i, 1 - 2 * core))
        for core in range(2)
        for i in range(n)
    ]
    return lax.ppermute(array, ("row", mesh_axis(axis)), pairs)


def shift(array, axis, step):
    pairs = [(i, shifted(axis, i, step)) for i in range(extent(axis))]
    return lax.ppermute(array, mesh_axis(axis), pairs)


def swap(array):
    return lax.ppermute(array, "row", [(0, 1), (1, 0)])


def ring(array, axis):
    pieces = [array]
    for _ in range(SIDE - 1):
        pieces.append(hop(pieces[-1], axis))
    return pieces


def join(pieces, core):
    flip = core == 1
    return jnp.concatenate(
        [
            pieces[0],
            jnp.where(flip, pieces[3], pieces[1]),
            pieces[2],
            jnp.where(flip, pieces[1], pieces[3]),
        ],
        axis=0,
    )


def gather(rows, core):
    panel_pieces = ring(rows, "x")
    third = rows.shape[0] // 3
    parts = []
    for part, (first, second) in enumerate((("y", "z"), ("z", "y"))):
        block = join([p[part * third : (part + 1) * third] for p in panel_pieces], core)
        parts.append(ring(join(ring(block, first), core), second))
    block = join(ring(rows[2 * third :], "y"), core)
    parts.append(ring(join(ring(block, "z"), core), "x"))
    return join(panel_pieces, core), [[part[k] for part in parts] for k in range(SIDE)]


def times_transpose(left, right):
    return lax.dot_general(left, right, (((1,), (1,)), ((), ())), preferred_element_type=F32)


def plain(left, right):
    return jnp.dot(left, right, preferred_element_type=F32)


def gate_up_grads(gate, up, hidden_grad):
    s = jax.nn.sigmoid(gate)
    grad_up = (hidden_grad * gate * s).astype(BF16)
    grad_gate = (hidden_grad * up * s * (1.0 + gate * (1.0 - s))).astype(BF16)
    return grad_gate, grad_up


def weight_grad_kernel(n_groups, n_parts, width, *refs):
    left = refs[:n_groups]
    right = refs[n_groups : n_groups + n_groups * n_parts]
    outs = refs[n_groups + n_groups * n_parts :]
    rows = right[0].shape[0]
    total = None
    for k in range(n_groups):
        for p in range(n_parts):
            term = jnp.dot(
                left[k][:, p * rows : (p + 1) * rows],
                right[k * n_parts + p][...],
                preferred_element_type=F32,
            )
            total = term if total is None else total + term
    if width is None:
        outs[0][...] = total.astype(BF16)
    else:
        half = total.shape[0] // 2
        outs[0][...] = total[:half].T[:, :width].astype(BF16)
        outs[1][...] = total[half:].T[:, :width].astype(BF16)


def weight_grad(left, right, width):
    n_groups, n_parts = len(left), len(right[0])
    flat = [piece for group in right for piece in group]
    rows, features = flat[0].shape
    block = 256
    hidden = left[0].shape[0]
    in_specs = [pl.BlockSpec(x.shape, lambda i: (0, 0)) for x in left]
    in_specs += [pl.BlockSpec((rows, block), lambda i: (0, i)) for _ in flat]
    if width is None:
        out_shape = [jax.ShapeDtypeStruct((hidden, features), BF16)]
        out_specs = [pl.BlockSpec((hidden, block), lambda i: (0, i))]
    else:
        out_shape = [jax.ShapeDtypeStruct((features, width), BF16)] * 2
        out_specs = [pl.BlockSpec((block, width), lambda i: (i, 0))] * 2
    tokens = rows * len(flat)
    return pl.pallas_call(
        lambda *refs: weight_grad_kernel(n_groups, n_parts, width, *refs),
        grid=(features // block,),
        in_specs=in_specs,
        out_specs=out_specs,
        out_shape=out_shape,
        cost_estimate=pl.CostEstimate(
            flops=2 * tokens * hidden * features,
            bytes_accessed=2 * tokens * (hidden + features) + 2 * hidden * features,
            transcendentals=0,
        ),
        compiler_params=pltpu.CompilerParams(vmem_limit_bytes=40 * 1024 * 1024),
    )(*left, *flat)


def slice_sum(product, rows):
    total = product[:rows].astype(F32)
    for back in range(1, N_COL):
        total = total + shift(product[back * rows : (back + 1) * rows], "x", -back).astype(F32)
    return total.astype(BF16)


def per_device(tokens, gate_weight, up_weight, down_weight, cotangent):
    core = lax.axis_index("row")
    depth = lax.axis_index("depth")
    rows = tokens.shape[0]
    hidden_width = gate_weight.shape[1]
    own = hidden_width // N_DEPTH
    wide = -(-own // 128) * 128

    def own_columns(weight):
        cut = lax.dynamic_slice_in_dim(weight, depth * own, own, axis=1)
        return jnp.pad(cut.T, ((0, wide - own), (0, 0)))

    own_gate_up = jnp.concatenate([own_columns(gate_weight), own_columns(up_weight)], axis=0)
    own_down = jnp.pad(
        lax.dynamic_slice_in_dim(down_weight, depth * own, own, axis=0), ((0, wide - own), (0, 0))
    )

    panel, token_groups = gather(tokens, core)
    grad_panel, grad_groups = gather(cotangent, core)

    partial = jnp.concatenate(
        [plain(panel, gate_weight), plain(panel, up_weight)], axis=1
    ).astype(BF16)
    joined = partial.astype(F32) + swap(partial).astype(F32)
    gate_vals, up_vals = joined[:, :hidden_width], joined[:, hidden_width:]
    hidden = (jax.nn.silu(gate_vals) * up_vals).astype(BF16)
    mixed = slice_sum(plain(hidden, down_weight).astype(BF16), rows)
    partial = times_transpose(grad_panel, down_weight).astype(BF16)
    hidden_grad = partial.astype(F32) + swap(partial).astype(F32)
    grad_gate, grad_up = gate_up_grads(gate_vals, up_vals, hidden_grad)
    input_grad = slice_sum(
        (times_transpose(grad_gate, gate_weight) + times_transpose(grad_up, up_weight)).astype(
            BF16
        ),
        rows,
    )

    def partials(weight, groups):
        return [
            jnp.concatenate([times_transpose(weight, piece) for piece in group], axis=1).astype(
                BF16
            )
            for group in groups
        ]

    def row_sums(parts):
        return [
            parts[k].astype(F32) + swap(parts[-k % SIDE]).astype(F32) for k in range(SIDE)
        ]

    all_gate_up = row_sums(partials(own_gate_up, token_groups))
    all_hidden_grad = row_sums(partials(own_down, grad_groups))
    all_hidden, all_grads = [], []
    for gate_up, one_grad in zip(all_gate_up, all_hidden_grad):
        gate, up = gate_up[:wide], gate_up[wide:]
        all_hidden.append((jax.nn.silu(gate) * up).astype(BF16))
        all_grads.append(jnp.concatenate(gate_up_grads(gate, up, one_grad), axis=0))

    (down_block,) = weight_grad(all_hidden, grad_groups, None)
    down_grad = lax.all_to_all(down_block[:own], "depth", split_axis=1, concat_axis=0, tiled=True)
    gate_grad, up_grad = weight_grad(all_grads, token_groups, own)
    return mixed, input_grad, gate_grad, up_grad, down_grad


def solution(mesh):
    placed = (
        P(("col", "depth"), "row"),
        P("row", "col"),
        P("row", "col"),
        P("col", "row"),
        P(("col", "depth"), "row"),
    )
    return jax.shard_map(
        per_device,
        mesh=mesh,
        in_specs=placed,
        out_specs=(
            P(("col", "depth"), "row"),
            P(("col", "depth"), "row"),
            P("row", ("col", "depth")),
            P("row", ("col", "depth")),
            P("col", ("row", "depth")),
        ),
        check_vma=False,
    )
```

```python
import jax
import jax.numpy as jnp
from jax import lax
from jax.experimental import pallas as pl
from jax.experimental.pallas import tpu as pltpu
from jax.sharding import PartitionSpec as P

N_COL = 4
N_DEPTH = 16
SIDE = 4
BF16 = jnp.bfloat16
F32 = jnp.float32
LAST = (((1,), (1,)), ((), ()))
MIB = 1024 * 1024


def shifted(axis, index, step):
    if axis == "x":
        return (index + step) % N_COL
    z, y = divmod(index, SIDE)
    if axis == "y":
        return z * SIDE + (y + step) % SIDE
    return ((z + step) % SIDE) * SIDE + y


def extent(axis):
    return N_COL if axis == "x" else N_DEPTH


def mesh_axis(axis):
    return "col" if axis == "x" else "depth"


def hop(array, axis):
    n = extent(axis)
    pairs = [
        (core * n + i, core * n + shifted(axis, i, 1 - 2 * core))
        for core in range(2)
        for i in range(n)
    ]
    return lax.ppermute(array, ("row", mesh_axis(axis)), pairs)


def shift(array, axis, step):
    pairs = [(i, shifted(axis, i, step)) for i in range(extent(axis))]
    return lax.ppermute(array, mesh_axis(axis), pairs)


def swap(array):
    return lax.ppermute(array, "row", [(0, 1), (1, 0)])


def tie(values, *deps):
    return lax.optimization_barrier((*values, *deps))[: len(values)]


def regroup_kernel(n_in, plan, *refs):
    for out_ref, rows in zip(refs[n_in:], plan):
        at = 0
        for source, start, count in rows:
            out_ref[at : at + count] = refs[source][start : start + count]
            at += count


def regroup(arrays, plan):
    features = arrays[0].shape[1]
    counts = [sum(count for _, _, count in rows) for rows in plan]
    return pl.pallas_call(
        lambda *refs: regroup_kernel(len(arrays), plan, *refs),
        out_shape=[jax.ShapeDtypeStruct((n, features), BF16) for n in counts],
        cost_estimate=cost(6),
        compiler_params=pltpu.CompilerParams(vmem_limit_bytes=16 * MIB),
    )(*arrays)


def times_transpose(left, right):
    return lax.dot_general(left, right, LAST, preferred_element_type=F32)


def plain(left, right):
    return jnp.dot(left, right, preferred_element_type=F32)


def gate_up_grads(gate, up, hidden_grad):
    s = jax.nn.sigmoid(gate)
    grad_up = (hidden_grad * gate * s).astype(BF16)
    grad_gate = (hidden_grad * up * s * (1.0 + gate * (1.0 - s))).astype(BF16)
    return grad_gate, grad_up


def cost(megabytes):
    return pl.CostEstimate(flops=0, bytes_accessed=int(megabytes * 1e6), transcendentals=0)


def all_rows(pieces):
    return jnp.concatenate([x[...].reshape(-1, x.shape[-1]) for x in pieces], axis=0)


def own_partials_kernel(n_parts, sides, *refs):
    weights, out_ref = refs[len(sides) * n_parts : -1], refs[-1]
    rows = out_ref.shape[1]
    at = 0
    for s, (side, weight_ref) in enumerate(zip(sides, weights)):
        left = all_rows(refs[s * n_parts : (s + 1) * n_parts])
        product = (times_transpose if side else plain)(left, weight_ref[...]).astype(BF16)
        width = product.shape[1]
        for p in range(n_parts):
            out_ref[p, :, at : at + width] = product[p * rows : (p + 1) * rows]
        at += width


def own_partials(pieces, weights, sides, steps=2):
    n_parts = len(pieces)
    blocks, _, n, features = pieces[0].shape
    used = [weights[side] for side in sides]
    widths = [w.shape[0] if side else w.shape[1] for side, w in zip(sides, used)]

    def spec(side):
        return pl.BlockSpec((blocks // steps, 1, n, features), lambda i: (i, side, 0, 0))

    return pl.pallas_call(
        lambda *refs: own_partials_kernel(n_parts, sides, *refs),
        grid=(steps,),
        in_specs=[spec(side) for side in sides for _ in pieces]
        + [pl.BlockSpec(w.shape, lambda i: (0, 0)) for w in used],
        out_specs=pl.BlockSpec((n_parts, blocks * n // steps, sum(widths)), lambda i: (0, i, 0)),
        out_shape=jax.ShapeDtypeStruct((n_parts, blocks * n, sum(widths)), BF16),
        cost_estimate=cost(10),
        compiler_params=pltpu.CompilerParams(vmem_limit_bytes=32 * MIB),
    )(*[x for _ in sides for x in pieces], *used)


def row_sum(mine_ref, theirs_ref):
    n = mine_ref.shape[1] // SIDE
    theirs = jnp.concatenate(
        [theirs_ref[0, (-k % SIDE) * n : (-k % SIDE + 1) * n] for k in range(SIDE)], axis=0
    )
    return mine_ref[0].astype(F32) + theirs.astype(F32)


def hidden_kernel(mine_ref, theirs_ref, out_ref):
    wide = out_ref.shape[0]
    total = row_sum(mine_ref, theirs_ref)
    gate, up = total[:, :wide], total[:, wide:]
    out_ref[...] = (gate * jax.nn.sigmoid(gate) * up).T.astype(BF16)


def grads_kernel(mine_ref, theirs_ref, mine_grad_ref, theirs_grad_ref, out_ref):
    wide = out_ref.shape[0] // 2
    total = row_sum(mine_ref, theirs_ref)
    gate, up = total[:, :wide], total[:, wide:]
    hidden_grad = row_sum(mine_grad_ref, theirs_grad_ref)
    s = jax.nn.sigmoid(gate)
    out_ref[:wide] = (hidden_grad * up * s * (1.0 + gate * (1.0 - s))).T.astype(BF16)
    out_ref[wide:] = (hidden_grad * gate * s).T.astype(BF16)


def activations(kernel, width, *args):
    n_parts, rows, _ = args[0][0].shape

    def spec(columns, block):
        return pl.BlockSpec((1, rows, columns), lambda i: (i, 0, block))

    return pl.pallas_call(
        kernel,
        grid=(n_parts,),
        in_specs=[spec(columns, block) for _, columns, block in args],
        out_specs=pl.BlockSpec((width, rows), lambda i: (0, i)),
        out_shape=jax.ShapeDtypeStruct((width, n_parts * rows), BF16),
        cost_estimate=cost(5),
        compiler_params=pltpu.CompilerParams(vmem_limit_bytes=32 * MIB),
    )(*[x for x, _, _ in args])


def weight_grad_kernel(n_groups, n_parts, before, own, kind, *refs):
    left = refs[:n_groups]
    right = refs[n_groups : n_groups + n_groups * n_parts]
    outs = refs[n_groups + n_groups * n_parts :]
    rows = right[0].shape[0] * right[0].shape[2]
    total = None
    if before:
        total, outs = outs[0][...], outs[1:]
    for k in range(n_groups):
        for p in range(n_parts):
            piece = right[k * n_parts + p][...].reshape(rows, -1)
            term = plain(left[k][:, p * rows : (p + 1) * rows], piece)
            total = term if total is None else total + term
    if kind == "sum":
        outs[0][...] = total
    elif kind == "blocks":
        width = outs[0].shape[2]
        for k in range(outs[0].shape[0]):
            outs[0][k] = total[:own, k * width : (k + 1) * width].astype(BF16)
    else:
        half = total.shape[0] // 2
        outs[0][...] = total[:own].astype(BF16)
        outs[1][...] = total[half : half + own].astype(BF16)


def weight_grad(left, right, side, kind, own, before=None, block=512):
    n_groups, n_parts = len(left), len(right[0])
    flat = [piece for group in right for piece in group]
    blocks, _, n, features = flat[0].shape
    hidden = left[0].shape[0]
    in_specs = [pl.BlockSpec(x.shape, lambda i: (0, 0)) for x in left]
    in_specs += [pl.BlockSpec((blocks, 1, n, block), lambda i: (0, side, 0, i)) for _ in flat]
    args = [*left, *flat]
    if before is not None:
        in_specs.append(pl.BlockSpec((hidden, block), lambda i: (0, i)))
        args.append(before)
    if kind == "sum":
        out_shape = [jax.ShapeDtypeStruct((hidden, features), F32)]
        out_specs = [pl.BlockSpec((hidden, block), lambda i: (0, i))]
    elif kind == "blocks":
        width = features // N_DEPTH
        out_shape = [jax.ShapeDtypeStruct((N_DEPTH, own, width), BF16)]
        out_specs = [pl.BlockSpec((block // width, own, width), lambda i: (i, 0, 0))]
    else:
        out_shape = [jax.ShapeDtypeStruct((own, features), BF16)] * 2
        out_specs = [pl.BlockSpec((own, block), lambda i: (0, i))] * 2
    return pl.pallas_call(
        lambda *refs: weight_grad_kernel(n_groups, n_parts, before is not None, own, kind, *refs),
        grid=(features // block,),
        in_specs=in_specs,
        out_specs=out_specs,
        out_shape=out_shape,
        cost_estimate=cost(18),
        compiler_params=pltpu.CompilerParams(vmem_limit_bytes=40 * MIB),
    )(*args)


def sums_at(refs, columns):
    return [
        mine[:, columns].astype(F32) + theirs[:, columns].astype(F32)
        for mine, theirs in zip(refs[::2], refs[1::2])
    ]


def mixed_kernel(*refs):
    weight_ref, out_ref, hidden_ref = refs[4:]

    @pl.when(pl.program_id(0) == 0)
    def _():
        for at in range(0, hidden_ref.shape[1], 512):
            columns = slice(at, at + 512)
            gate, up = sums_at(refs[:4], columns)
            hidden_ref[:, columns] = (gate * jax.nn.sigmoid(gate) * up).astype(BF16)

    out_ref[...] = plain(hidden_ref[...], weight_ref[...]).astype(BF16)


def whole(array):
    return pl.BlockSpec(array.shape, lambda i: (0, 0))


def mixed_product(gate_up, weight, block=512):
    width, features = weight.shape
    tokens = gate_up[0].shape[0]
    return pl.pallas_call(
        mixed_kernel,
        grid=(features // block,),
        in_specs=[*map(whole, gate_up), pl.BlockSpec((width, block), lambda i: (0, i))],
        out_specs=pl.BlockSpec((tokens, block), lambda i: (0, i)),
        out_shape=jax.ShapeDtypeStruct((tokens, features), BF16),
        scratch_shapes=[pltpu.VMEM((tokens, width), BF16)],
        cost_estimate=cost(28),
        compiler_params=pltpu.CompilerParams(vmem_limit_bytes=40 * MIB),
    )(*gate_up, weight)


def input_kernel(*refs):
    gate_ref, up_ref, out_ref, grad_gate_ref, grad_up_ref = refs[6:]

    @pl.when(pl.program_id(0) == 0)
    def _():
        for at in range(0, grad_gate_ref.shape[1], 512):
            columns = slice(at, at + 512)
            grad_gate_ref[:, columns], grad_up_ref[:, columns] = gate_up_grads(
                *sums_at(refs[:6], columns)
            )

    total = times_transpose(grad_gate_ref[...], gate_ref[...])
    total += times_transpose(grad_up_ref[...], up_ref[...])
    out_ref[...] = total.astype(BF16)


def input_product(values, gate_weight, up_weight, block=256):
    features, width = gate_weight.shape
    tokens = values[0].shape[0]
    rows = pl.BlockSpec((block, width), lambda i: (i, 0))
    return pl.pallas_call(
        input_kernel,
        grid=(features // block,),
        in_specs=[*map(whole, values), rows, rows],
        out_specs=pl.BlockSpec((tokens, block), lambda i: (0, i)),
        out_shape=jax.ShapeDtypeStruct((tokens, features), BF16),
        scratch_shapes=[pltpu.VMEM((tokens, width), BF16)] * 2,
        cost_estimate=cost(55),
        compiler_params=pltpu.CompilerParams(vmem_limit_bytes=40 * MIB),
    )(*values, gate_weight, up_weight)


def added(terms, start, count):
    total = terms[0][start : start + count].astype(F32)
    for term in terms[1:]:
        total = total + term[start : start + count].astype(F32)
    return total.astype(BF16)


def per_device(tokens, gate_weight, up_weight, down_weight, cotangent):
    depth = lax.axis_index("depth")
    rows = tokens.shape[0]
    hidden_width = gate_weight.shape[1]
    own = hidden_width // N_DEPTH
    wide = -(-own // 128) * 128

    n = rows // 3
    thirds = [[(0, p * n, n), (1, p * n, n)] for p in range(3)]
    mine, last = regroup([tokens, cotangent], [thirds[0] + thirds[1] + thirds[2], thirds[2]])
    xs = [mine] + [shift(mine, "x", s) for s in (1, 2, -1)]
    ys = [last] + [shift(last, "y", s) for s in (1, 2, -1)]

    panel_plan = [[(i, 2 * n * p + n * c, n) for i in range(4) for p in range(3)] for c in range(2)]
    part_plan = [[(i, 2 * n * p, 2 * n) for i in range(4)] for p in range(2)]
    panel, grad_panel, r0, t0 = regroup(xs, panel_plan + part_plan)
    r1, t1 = hop(r0, "y"), hop(t0, "z")
    q0 = jnp.concatenate(ys, axis=0)
    q1 = hop(q0, "z")

    (panel_,) = tie((panel,), q0)
    gate_part = plain(panel_, gate_weight).astype(BF16)
    (panel_,) = tie((panel,), gate_part, r1, t1, q1)
    (r1_, t1_, q1_) = tie((r1, t1, q1), gate_part)
    r2, t2, q2 = hop(r1_, "y"), hop(t1_, "z"), hop(q1_, "z")
    up_part = plain(panel_, up_weight).astype(BF16)
    gate_theirs = swap(gate_part)

    (grad_panel,) = tie((grad_panel,), up_part, r2, t2, q2)
    (r2_, t2_, q2_) = tie((r2, t2, q2), up_part)
    r3, t3, q3 = hop(r2_, "y"), hop(t2_, "z"), hop(q2_, "z")
    up_theirs = swap(up_part)
    grad_part = times_transpose(grad_panel, down_weight).astype(BF16)
    grad_theirs = swap(grad_part)

    r0, t0, q0 = tie((r0, t0, q0), grad_part)
    g0 = jnp.concatenate([r0, r1, r2, r3], axis=0)
    f0 = jnp.concatenate([t0, t1, t2, t3], axis=0)
    e0 = jnp.concatenate([q0, q1, q2, q3], axis=0)
    g1, f1, e1 = hop(g0, "z"), hop(f0, "y"), hop(e0, "x")
    (gate_part,) = tie((gate_part,), g0, f0, e0)
    gate_up = (gate_part, gate_theirs, up_part, up_theirs)
    mixed_part = mixed_product(gate_up, down_weight)
    (grad_part,) = tie((grad_part,), mixed_part)
    input_part = input_product((*gate_up, grad_part, grad_theirs), gate_weight, up_weight)

    def split(*arrays):
        return [x.reshape(-1, 2, n, x.shape[1]) for x in arrays]

    (depth,) = tie((depth,), input_part)

    def own_columns(weight):
        cut = lax.dynamic_slice_in_dim(weight, depth * own, own, axis=1)
        return jnp.pad(cut, ((0, 0), (0, wide - own)))

    own_gate_up = jnp.concatenate([own_columns(gate_weight), own_columns(up_weight)], axis=1)
    own_down = jnp.pad(
        lax.dynamic_slice_in_dim(down_weight, depth * own, own, axis=0), ((0, wide - own), (0, 0))
    )
    weights = (own_gate_up, own_down)
    pieces = [split(g0, f0, e0)]
    (p0, *_) = tie(pieces[0], input_part, g1, f1, e1)
    (g1_, f1_, e1_) = tie((g1, f1, e1), input_part)
    g2, f2, e2 = hop(g1_, "z"), hop(f1_, "y"), hop(e1_, "x")
    u0 = own_partials([p0, *pieces[0][1:]], weights, (0, 1))
    v0 = swap(u0)
    pieces.append(split(g1, f1, e1))
    (p1, *_) = tie(pieces[1], u0)
    u1 = own_partials([p1, *pieces[1][1:]], weights, (0, 1))
    v1 = swap(u1)

    pieces.append(split(g2, f2, e2))
    (p2, *_) = tie(pieces[2], u1)
    (g2_, f2_, e2_) = tie((g2, f2, e2), u1)
    g3, f3, e3 = hop(g2_, "z"), hop(f2_, "y"), hop(e2_, "x")
    u2 = own_partials([p2, *pieces[2][1:]], weights, (0, 1))
    v2 = swap(u2)

    def hidden_of(mine, theirs):
        return activations(hidden_kernel, wide, *[(x, 2 * wide, 0) for x in (mine, theirs)])

    def grads_of(mine, theirs, *grads):
        pre = [(x, 2 * wide, 0) for x in (mine, theirs)]
        return activations(grads_kernel, 2 * wide, *pre, *[(x, wide, at) for x, at in grads])

    (u0,) = tie((u0,), u2)
    h0 = hidden_of(u0, v0)
    d0 = grads_of(u0, v0, (u0, 2), (v0, 2))
    (u2,) = tie((u2,), d0)
    h2 = hidden_of(u2, v2)
    d2 = grads_of(u2, v2, (u2, 2), (v2, 2))
    early = [pieces[0], pieces[2]]
    (down_early,) = weight_grad([h0, h2], early, 1, "sum", own)
    (d0,) = tie((d0,), down_early)
    (grads_early,) = weight_grad([d0, d2], early, 0, "sum", own)

    pieces.append(split(g3, f3, e3))

    def terms_of(back, *deps):
        plan = [(p, back * rows, rows) for p in range(2)]
        return regroup([mixed_part, input_part], [plan])

    (sums,) = zip(*[terms_of(back) for back in range(N_COL)])
    sums = tie(sums, grads_early, e3)
    sums = [sums[0]] + [shift(sums[back], "x", -back) for back in range(1, N_COL)]
    late = [pieces[1], pieces[3]]
    (p3, *_) = tie(pieces[3], grads_early)
    u3 = own_partials([p3, *pieces[3][1:]], weights, (0,))
    v3 = swap(u3)
    h3 = hidden_of(u3, v1)
    (u1,) = tie((u1,), h3)
    h1 = hidden_of(u1, v3)
    (down_blocks,) = weight_grad([h1, h3], late, 1, "blocks", own, before=down_early)
    down_grad = lax.all_to_all(down_blocks, "depth", split_axis=0, concat_axis=0, tiled=True)
    (p3, *_) = tie(pieces[3], h3)
    w3 = own_partials([p3, *pieces[3][1:]], weights, (1,))
    z3 = swap(w3)
    (u3,) = tie((u3,), down_blocks)
    d3 = grads_of(u3, v1, (w3, 0), (v1, 2))
    d1 = grads_of(u1, v3, (u1, 2), (z3, 0))
    gate_grad, up_grad = weight_grad([d1, d3], late, 0, "pair", own, before=grads_early)
    down_grad = down_grad.reshape(hidden_width, -1)
    sums = tie(tuple(sums), d1)
    mixed, input_grad = added(sums, 0, rows), added(sums, rows, rows)
    return mixed, input_grad, gate_grad.T, up_grad.T, down_grad


def solution(mesh):
    placed = (
        P(("col", "depth"), "row"),
        P("row", "col"),
        P("row", "col"),
        P("col", "row"),
        P(("col", "depth"), "row"),
    )
    return jax.shard_map(
        per_device,
        mesh=mesh,
        in_specs=placed,
        out_specs=(
            P(("col", "depth"), "row"),
            P(("col", "depth"), "row"),
            P("row", ("col", "depth")),
            P("row", ("col", "depth")),
            P("col", ("row", "depth")),
        ),
        check_vma=False,
    )
```

```python
import functools

import jax
import jax.numpy as jnp
from jax import lax
from jax.experimental import pallas as pl
from jax.experimental.pallas import tpu as pltpu
from jax.sharding import PartitionSpec as P

N_COL = 4
N_DEPTH = 16
SIDE = 4
PIECE = 256
BF16 = jnp.bfloat16
F32 = jnp.float32
LAST = (((1,), (1,)), ((), ()))
MIB = 1024 * 1024


def shifted(axis, index, step):
    if axis == "x":
        return (index + step) % N_COL
    z, y = divmod(index, SIDE)
    if axis == "y":
        return z * SIDE + (y + step) % SIDE
    return ((z + step) % SIDE) * SIDE + y


def extent(axis):
    return N_COL if axis == "x" else N_DEPTH


def mesh_axis(axis):
    return "col" if axis == "x" else "depth"


def hop(array, axis):
    n = extent(axis)
    pairs = [
        (core * n + i, core * n + shifted(axis, i, 1 - 2 * core))
        for core in range(2)
        for i in range(n)
    ]
    return lax.ppermute(array, ("row", mesh_axis(axis)), pairs)


def shift(array, axis, step):
    pairs = [(i, shifted(axis, i, step)) for i in range(extent(axis))]
    return lax.ppermute(array, mesh_axis(axis), pairs)


def swap(array):
    return lax.ppermute(array, "row", [(0, 1), (1, 0)])


def ring(array, axis):
    pieces = [array]
    for _ in range(SIDE - 1):
        pieces.append(hop(pieces[-1], axis))
    return pieces


def tie(values, *deps):
    return lax.optimization_barrier((*values, *deps))[: len(values)]


def regroup_kernel(n_in, plans, core_ref, *refs):
    def copy(plan):
        for out_ref, rows in zip(refs[n_in:], plan):
            at = 0
            for source, start, count in rows:
                out_ref[at : at + count] = refs[source][start : start + count]
                at += count

    if len(plans) == 1:
        copy(plans[0])
    else:
        for c, plan in enumerate(plans):
            pl.when(core_ref[0] == c)(functools.partial(copy, plan))


def regroup(core, arrays, *plans):
    features = arrays[0].shape[1]
    counts = [sum(count for _, _, count in rows) for rows in plans[0]]
    return pl.pallas_call(
        lambda *refs: regroup_kernel(len(arrays), plans, *refs),
        in_specs=[pl.BlockSpec(memory_space=pltpu.SMEM)]
        + [pl.BlockSpec(memory_space=pltpu.VMEM)] * len(arrays),
        out_shape=[jax.ShapeDtypeStruct((n, features), BF16) for n in counts],
        cost_estimate=cost(1),
        compiler_params=pltpu.CompilerParams(vmem_limit_bytes=16 * MIB),
    )(core, *arrays)


def times_transpose(left, right):
    return lax.dot_general(left, right, LAST, preferred_element_type=F32)


def plain(left, right):
    return jnp.dot(left, right, preferred_element_type=F32)


def gate_up_grads(gate, up, hidden_grad):
    s = jax.nn.sigmoid(gate)
    grad_up = (hidden_grad * gate * s).astype(BF16)
    grad_gate = (hidden_grad * up * s * (1.0 + gate * (1.0 - s))).astype(BF16)
    return grad_gate, grad_up


def cost(megabytes):
    return pl.CostEstimate(flops=0, bytes_accessed=int(megabytes * 1e6), transcendentals=0)


def own_partials_kernel(n_parts, sides, *refs):
    weights, out_ref = refs[len(sides) * n_parts : -1], refs[-1]
    rows = out_ref.shape[1]
    at = 0
    for s, (side, weight_ref) in enumerate(zip(sides, weights)):
        left = jnp.concatenate([x[...] for x in refs[s * n_parts : (s + 1) * n_parts]], axis=0)
        product = (times_transpose if side else plain)(left, weight_ref[...]).astype(BF16)
        width = product.shape[1]
        for p in range(n_parts):
            out_ref[p, :, at : at + width] = product[p * rows : (p + 1) * rows]
        at += width


def own_partials(pieces, weights, sides, steps=2):
    n_parts = len(pieces[0])
    flat = [x for side in pieces for x in side]
    rows, features = PIECE, flat[0][0].shape[1]
    used = [weights[side] for side in sides]
    widths = [w.shape[0] if side else w.shape[1] for side, w in zip(sides, used)]

    def spec(at):
        return pl.BlockSpec((rows // steps, features), lambda i: (at * steps + i, 0))

    return pl.pallas_call(
        lambda *refs: own_partials_kernel(n_parts, sides, *refs),
        grid=(steps,),
        in_specs=[spec(at) for _, at in flat]
        + [pl.BlockSpec(w.shape, lambda i: (0, 0)) for w in used],
        out_specs=pl.BlockSpec((n_parts, rows // steps, sum(widths)), lambda i: (0, i, 0)),
        out_shape=jax.ShapeDtypeStruct((n_parts, rows, sum(widths)), BF16),
        cost_estimate=cost(1),
        compiler_params=pltpu.CompilerParams(vmem_limit_bytes=32 * MIB),
    )(*[x for x, _ in flat], *used)


def row_sum(mine_ref, theirs_ref):
    n = mine_ref.shape[1] // SIDE
    theirs = jnp.concatenate(
        [theirs_ref[0, (-k % SIDE) * n : (-k % SIDE + 1) * n] for k in range(SIDE)], axis=0
    )
    return mine_ref[0].astype(F32) + theirs.astype(F32)


def hidden_kernel(mine_ref, theirs_ref, out_ref):
    wide = out_ref.shape[0]
    total = row_sum(mine_ref, theirs_ref)
    gate, up = total[:, :wide], total[:, wide:]
    out_ref[...] = (gate * jax.nn.sigmoid(gate) * up).T.astype(BF16)


def grads_kernel(mine_ref, theirs_ref, mine_grad_ref, theirs_grad_ref, out_ref):
    wide = out_ref.shape[0] // 2
    total = row_sum(mine_ref, theirs_ref)
    gate, up = total[:, :wide], total[:, wide:]
    hidden_grad = row_sum(mine_grad_ref, theirs_grad_ref)
    s = jax.nn.sigmoid(gate)
    out_ref[:wide] = (hidden_grad * up * s * (1.0 + gate * (1.0 - s))).T.astype(BF16)
    out_ref[wide:] = (hidden_grad * gate * s).T.astype(BF16)


def activations(kernel, width, *args):
    n_parts, rows, _ = args[0][0].shape

    def spec(columns, block):
        return pl.BlockSpec((1, rows, columns), lambda i: (i, 0, block))

    return pl.pallas_call(
        kernel,
        grid=(n_parts,),
        in_specs=[spec(columns, block) for _, columns, block in args],
        out_specs=pl.BlockSpec((width, rows), lambda i: (0, i)),
        out_shape=jax.ShapeDtypeStruct((width, n_parts * rows), BF16),
        cost_estimate=cost(1),
        compiler_params=pltpu.CompilerParams(vmem_limit_bytes=32 * MIB),
    )(*[x for x, _, _ in args])


def weight_grad_kernel(n_groups, n_parts, before, own, kind, *refs):
    left = refs[:n_groups]
    right = refs[n_groups : n_groups + n_groups * n_parts]
    outs = refs[n_groups + n_groups * n_parts :]
    rows = right[0].shape[0]
    total = None
    if before:
        total, outs = outs[0][...], outs[1:]
    for k in range(n_groups):
        for p in range(n_parts):
            term = plain(left[k][:, p * rows : (p + 1) * rows], right[k * n_parts + p][...])
            total = term if total is None else total + term
    if kind == "sum":
        outs[0][...] = total
    elif kind == "blocks":
        width = outs[0].shape[2]
        for k in range(outs[0].shape[0]):
            outs[0][k] = total[:own, k * width : (k + 1) * width].astype(BF16)
    else:
        half = total.shape[0] // 2
        outs[0][...] = total[:own].astype(BF16)
        outs[1][...] = total[half : half + own].astype(BF16)


def weight_grad(left, right, kind, own, before=None, block=512):
    n_groups, n_parts = len(left), len(right[0])
    flat = [piece for group in right for piece in group]
    rows, features = PIECE, flat[0][0].shape[1]
    hidden = left[0].shape[0]

    def spec(at):
        return pl.BlockSpec((rows, block), lambda i: (at, i))

    in_specs = [pl.BlockSpec(x.shape, lambda i: (0, 0)) for x in left]
    in_specs += [spec(at) for _, at in flat]
    args = [*left, *[x for x, _ in flat]]
    if before is not None:
        in_specs.append(pl.BlockSpec((hidden, block), lambda i: (0, i)))
        args.append(before)
    if kind == "sum":
        out_shape = [jax.ShapeDtypeStruct((hidden, features), F32)]
        out_specs = [pl.BlockSpec((hidden, block), lambda i: (0, i))]
    elif kind == "blocks":
        width = features // N_DEPTH
        out_shape = [jax.ShapeDtypeStruct((N_DEPTH, own, width), BF16)]
        out_specs = [pl.BlockSpec((block // width, own, width), lambda i: (i, 0, 0))]
    else:
        out_shape = [jax.ShapeDtypeStruct((own, features), BF16)] * 2
        out_specs = [pl.BlockSpec((own, block), lambda i: (0, i))] * 2
    return pl.pallas_call(
        lambda *refs: weight_grad_kernel(n_groups, n_parts, before is not None, own, kind, *refs),
        grid=(features // block,),
        in_specs=in_specs,
        out_specs=out_specs,
        out_shape=out_shape,
        cost_estimate=cost(1),
        compiler_params=pltpu.CompilerParams(vmem_limit_bytes=40 * MIB),
    )(*args)


def sums_at(refs, columns):
    return [
        mine[:, columns].astype(F32) + theirs[:, columns].astype(F32)
        for mine, theirs in zip(refs[::2], refs[1::2])
    ]


def mixed_kernel(*refs):
    weight_ref, out_ref, hidden_ref = refs[4:]

    @pl.when(pl.program_id(0) == 0)
    def _():
        for at in range(0, hidden_ref.shape[1], 512):
            columns = slice(at, at + 512)
            gate, up = sums_at(refs[:4], columns)
            hidden_ref[:, columns] = (gate * jax.nn.sigmoid(gate) * up).astype(BF16)

    out_ref[...] = plain(hidden_ref[...], weight_ref[...]).astype(BF16)


def whole(array):
    return pl.BlockSpec(array.shape, lambda i: (0, 0))


def mixed_product(gate_up, weight, block=512):
    width, features = weight.shape
    tokens = gate_up[0].shape[0]
    return pl.pallas_call(
        mixed_kernel,
        grid=(features // block,),
        in_specs=[*map(whole, gate_up), pl.BlockSpec((width, block), lambda i: (0, i))],
        out_specs=pl.BlockSpec((tokens, block), lambda i: (0, i)),
        out_shape=jax.ShapeDtypeStruct((tokens, features), BF16),
        scratch_shapes=[pltpu.VMEM((tokens, width), BF16)],
        cost_estimate=cost(1),
        compiler_params=pltpu.CompilerParams(vmem_limit_bytes=52 * MIB),
    )(*gate_up, weight)


def input_kernel(*refs):
    gate_ref, up_ref, out_ref, grad_gate_ref, grad_up_ref = refs[6:]

    @pl.when(pl.program_id(0) == 0)
    def _():
        for at in range(0, grad_gate_ref.shape[1], 512):
            columns = slice(at, at + 512)
            grad_gate_ref[:, columns], grad_up_ref[:, columns] = gate_up_grads(
                *sums_at(refs[:6], columns)
            )

    total = times_transpose(grad_gate_ref[...], gate_ref[...])
    total += times_transpose(grad_up_ref[...], up_ref[...])
    out_ref[...] = total.astype(BF16)


def input_product(values, gate_weight, up_weight, block=256):
    features, width = gate_weight.shape
    tokens = values[0].shape[0]
    rows = pl.BlockSpec((block, width), lambda i: (i, 0))
    return pl.pallas_call(
        input_kernel,
        grid=(features // block,),
        in_specs=[*map(whole, values), rows, rows],
        out_specs=pl.BlockSpec((tokens, block), lambda i: (0, i)),
        out_shape=jax.ShapeDtypeStruct((tokens, features), BF16),
        scratch_shapes=[pltpu.VMEM((tokens, width), BF16)] * 2,
        cost_estimate=cost(1),
        compiler_params=pltpu.CompilerParams(vmem_limit_bytes=52 * MIB),
    )(*values, gate_weight, up_weight)


def added(terms, start, count):
    total = terms[0][start : start + count].astype(F32)
    for term in terms[1:]:
        total = total + term[start : start + count].astype(F32)
    return total.astype(BF16)


def per_device(tokens, gate_weight, up_weight, down_weight, cotangent):
    core = lax.axis_index("row").astype(jnp.int32).reshape(1)
    depth = lax.axis_index("depth")
    rows = tokens.shape[0]
    hidden_width = gate_weight.shape[1]
    own = hidden_width // N_DEPTH
    wide = -(-own // 128) * 128

    n = rows // 3
    thirds = [[(0, p * n, n), (1, p * n, n)] for p in range(3)]
    mine, zs, ys = regroup(
        core, [tokens, cotangent], [thirds[0] + thirds[1] + thirds[2], thirds[1], thirds[2]]
    )
    xs = [mine] + [shift(mine, "x", s) for s in (1, 2, -1)]
    zs, ys = ring(zs, "z"), ring(ys, "y")

    def joined(pieces, half):
        orders = ((0, 1, 2, 3), (0, 3, 2, 1))
        plans = [[[(i, c * half, half) for c in range(2) for i in order]] for order in orders]
        return regroup(core, pieces, *plans)[0]

    def stacked(pieces, half):
        return regroup(core, pieces, [[(i, c * half, half) for c in range(2) for i in range(4)]])[0]

    panel_plan = [[(i, 2 * n * p + n * c, n) for i in range(4) for p in range(3)] for c in range(2)]
    first_plan = [(i, n * c, n) for c in range(2) for i in range(4)]
    panel, grad_panel, r0 = regroup(core, xs, [*panel_plan, first_plan])
    t0, q0 = joined(zs, n), joined(ys, n)
    r1, t1, q1 = hop(r0, "y"), hop(t0, "x"), hop(q0, "z")

    def own_columns(weight):
        cut = lax.dynamic_slice_in_dim(weight, depth * own, own, axis=1)
        return jnp.pad(cut, ((0, 0), (0, wide - own)))

    own_gate_up = jnp.concatenate([own_columns(gate_weight), own_columns(up_weight)], axis=1)
    own_down = jnp.pad(
        lax.dynamic_slice_in_dim(down_weight, depth * own, own, axis=0), ((0, wide - own), (0, 0))
    )

    (panel_,) = tie((panel,), r0, t0, q0, own_gate_up, own_down)
    gate_part = plain(panel_, gate_weight).astype(BF16)

    (panel_,) = tie((panel,), gate_part, r1, t1, q1)
    (r1_, t1_, q1_) = tie((r1, t1, q1), gate_part)
    r2, t2, q2 = hop(r1_, "y"), hop(t1_, "x"), hop(q1_, "z")
    up_part = plain(panel_, up_weight).astype(BF16)
    gate_theirs = swap(gate_part)

    (grad_panel,) = tie((grad_panel,), up_part, r2, t2, q2, gate_theirs)
    (r2_, t2_, q2_) = tie((r2, t2, q2), up_part)
    r3, t3, q3 = hop(r2_, "y"), hop(t2_, "x"), hop(q2_, "z")
    up_theirs = swap(up_part)
    grad_part = times_transpose(grad_panel, down_weight).astype(BF16)

    r0, r1, r2, r3 = tie((r0, r1, r2, r3), grad_part, up_theirs)
    t0, t1, t2, t3 = tie((t0, t1, t2, t3), grad_part)
    grad_theirs = swap(grad_part)
    q0, q1, q2, q3 = tie((q0, q1, q2, q3), grad_part, grad_theirs)
    axes = ("z", "y", "x")

    def hops(pieces, *deps):
        return [hop(*tie((x,), *deps), axis) for x, axis in zip(pieces, axes)]

    both = [[stacked(x, 4 * n) for x in ((r0, r1, r2, r3), (t0, t1, t2, t3), (q0, q1, q2, q3))]]
    both.append(hops(both[0]))
    (gate_part,) = tie((gate_part,), *both[0])
    gate_up = (gate_part, gate_theirs, up_part, up_theirs)
    input_part = input_product((*gate_up, grad_part, grad_theirs), gate_weight, up_weight)

    both.append(hops(both[1], input_part))
    (gate_part,) = tie((gate_part,), input_part, *both[1])
    mixed_part = mixed_product((gate_part, *gate_up[1:]), down_weight)
    (own_down_,) = tie((own_down,), mixed_part)
    toks = [[(x, 0) for x in pieces] for pieces in both[:2]]
    cots = [[(x, 1) for x in pieces] for pieces in both[:2]]
    u0 = own_partials([toks[0], cots[0]], (own_gate_up, own_down_), (0, 1))
    v0 = swap(u0)
    (own_down_,) = tie((own_down,), u0)
    u1 = own_partials([toks[1], cots[1]], (own_gate_up, own_down_), (0, 1))
    v1 = swap(u1)
    back_plan = [[(p, back * rows, rows) for p in range(2)] for back in range(N_COL)]
    sums = regroup(core, [mixed_part, input_part], back_plan)

    both.append(hops(both[2], u1, v0, v1, *sums))
    toks.append([(x, 0) for x in both[2]])
    cots.append([(x, 1) for x in both[2]])
    (own_down_,) = tie((own_down,), u1, *both[2])
    u2 = own_partials([toks[2], cots[2]], (own_gate_up, own_down_), (0, 1))
    v2 = swap(u2)

    def hidden_of(mine, theirs):
        return activations(hidden_kernel, wide, *[(x, 2 * wide, 0) for x in (mine, theirs)])

    def grads_of(mine, theirs, *grads):
        pre = [(x, 2 * wide, 0) for x in (mine, theirs)]
        return activations(grads_kernel, 2 * wide, *pre, *[(x, wide, at) for x, at in grads])

    (u0,) = tie((u0,), u2)
    h0 = hidden_of(u0, v0)
    d0 = grads_of(u0, v0, (u0, 2), (v0, 2))
    (u2,) = tie((u2,), d0)
    h2 = hidden_of(u2, v2)
    d2 = grads_of(u2, v2, (u2, 2), (v2, 2))
    (h2,) = tie((h2,), d2)
    (down_early,) = weight_grad([h0, h2], [cots[0], cots[2]], "sum", own)
    (d2,) = tie((d2,), down_early)
    (grads_early,) = weight_grad([d0, d2], [toks[0], toks[2]], "sum", own)

    toks.append([(x, 0) for x in both[3]])
    cots.append([(x, 1) for x in both[3]])
    (own_gate_up_,) = tie((own_gate_up,), grads_early, *both[3])
    u3 = own_partials([toks[3]], (own_gate_up_, None), (0,))
    v3 = swap(u3)
    h3 = hidden_of(u3, v1)
    (u1,) = tie((u1,), h3)
    h1 = hidden_of(u1, v3)
    (down_blocks,) = weight_grad([h1, h3], [cots[1], cots[3]], "blocks", own, before=down_early)
    down_grad = lax.all_to_all(down_blocks, "depth", split_axis=0, concat_axis=0, tiled=True)

    (own_down_,) = tie((own_down,), h3)
    w3 = own_partials([cots[3]], (None, own_down_), (1,))
    z3 = swap(w3)
    (u3,) = tie((u3,), down_blocks)
    d3 = grads_of(u3, v1, (w3, 0), (v1, 2))
    sums = tie(tuple(sums), d3)
    sums = [sums[0]] + [shift(sums[back], "x", -back) for back in range(1, N_COL)]
    d1 = grads_of(u1, v3, (u1, 2), (z3, 0))
    gate_grad, up_grad = weight_grad(
        [d1, d3], [toks[1], toks[3]], "pair", own, before=grads_early
    )
    down_grad = down_grad.reshape(hidden_width, -1)
    sums = tie(tuple(sums), gate_grad)
    mixed, input_grad = added(sums, 0, rows), added(sums, rows, rows)
    return mixed, input_grad, gate_grad.T, up_grad.T, down_grad


def solution(mesh):
    placed = (
        P(("col", "depth"), "row"),
        P("row", "col"),
        P("row", "col"),
        P("col", "row"),
        P(("col", "depth"), "row"),
    )
    return jax.shard_map(
        per_device,
        mesh=mesh,
        in_specs=placed,
        out_specs=(
            P(("col", "depth"), "row"),
            P(("col", "depth"), "row"),
            P("row", ("col", "depth")),
            P("row", ("col", "depth")),
            P("col", ("row", "depth")),
        ),
        check_vma=False,
    )
```

```python
import functools

import jax
import jax.numpy as jnp
from jax import lax
from jax.experimental import pallas as pl
from jax.experimental.pallas import tpu as pltpu
from jax.sharding import PartitionSpec as P

N_COL = 4
N_DEPTH = 16
SIDE = 4
PIECE = 256
BF16 = jnp.bfloat16
F32 = jnp.float32
LAST = (((1,), (1,)), ((), ()))
MIB = 1024 * 1024


def shifted(axis, index, step):
    if axis == "x":
        return (index + step) % N_COL
    z, y = divmod(index, SIDE)
    if axis == "y":
        return z * SIDE + (y + step) % SIDE
    return ((z + step) % SIDE) * SIDE + y


def extent(axis):
    return N_COL if axis == "x" else N_DEPTH


def mesh_axis(axis):
    return "col" if axis == "x" else "depth"


def hop(array, axis):
    n = extent(axis)
    pairs = [
        (core * n + i, core * n + shifted(axis, i, 1 - 2 * core))
        for core in range(2)
        for i in range(n)
    ]
    return lax.ppermute(array, ("row", mesh_axis(axis)), pairs)


def shift(array, axis, step):
    pairs = [(i, shifted(axis, i, step)) for i in range(extent(axis))]
    return lax.ppermute(array, mesh_axis(axis), pairs)


def swap(array):
    return lax.ppermute(array, "row", [(0, 1), (1, 0)])


def ring(array, axis):
    pieces = [array]
    for _ in range(SIDE - 1):
        pieces.append(hop(pieces[-1], axis))
    return pieces


def tie(values, *deps):
    return lax.optimization_barrier((*values, *deps))[: len(values)]


def regroup_kernel(n_in, plans, core_ref, *refs):
    def copy(plan):
        for out_ref, rows in zip(refs[n_in:], plan):
            at = 0
            for source, start, count in rows:
                out_ref[at : at + count] = refs[source][start : start + count]
                at += count

    if len(plans) == 1:
        copy(plans[0])
    else:
        for c, plan in enumerate(plans):
            pl.when(core_ref[0] == c)(functools.partial(copy, plan))


def regroup(core, arrays, *plans):
    features = arrays[0].shape[1]
    counts = [sum(count for _, _, count in rows) for rows in plans[0]]
    return pl.pallas_call(
        lambda *refs: regroup_kernel(len(arrays), plans, *refs),
        in_specs=[pl.BlockSpec(memory_space=pltpu.SMEM)]
        + [pl.BlockSpec(memory_space=pltpu.VMEM)] * len(arrays),
        out_shape=[jax.ShapeDtypeStruct((n, features), BF16) for n in counts],
        cost_estimate=cost(1),
        compiler_params=pltpu.CompilerParams(vmem_limit_bytes=16 * MIB),
    )(core, *arrays)


def times_transpose(left, right):
    return lax.dot_general(left, right, LAST, preferred_element_type=F32)


def plain(left, right):
    return jnp.dot(left, right, preferred_element_type=F32)


def gate_up_grads(gate, up, hidden_grad):
    s = jax.nn.sigmoid(gate)
    grad_up = (hidden_grad * gate * s).astype(BF16)
    grad_gate = (hidden_grad * up * s * (1.0 + gate * (1.0 - s))).astype(BF16)
    return grad_gate, grad_up


def cost(megabytes):
    return pl.CostEstimate(flops=0, bytes_accessed=int(megabytes * 1e6), transcendentals=0)


def own_partials_kernel(n_parts, sides, *refs):
    weights, out_ref = refs[len(sides) * n_parts : -1], refs[-1]
    rows = out_ref.shape[1]
    at = 0
    for s, (side, weight_ref) in enumerate(zip(sides, weights)):
        left = jnp.concatenate([x[...] for x in refs[s * n_parts : (s + 1) * n_parts]], axis=0)
        product = (times_transpose if side else plain)(left, weight_ref[...]).astype(BF16)
        width = product.shape[1]
        for p in range(n_parts):
            out_ref[p, :, at : at + width] = product[p * rows : (p + 1) * rows]
        at += width


def own_partials(pieces, weights, sides, steps=2):
    n_parts = len(pieces[0])
    flat = [x for side in pieces for x in side]
    rows, features = PIECE, flat[0][0].shape[1]
    used = [weights[side] for side in sides]
    widths = [w.shape[0] if side else w.shape[1] for side, w in zip(sides, used)]

    def spec(at):
        return pl.BlockSpec((rows // steps, features), lambda i: (at * steps + i, 0))

    return pl.pallas_call(
        lambda *refs: own_partials_kernel(n_parts, sides, *refs),
        grid=(steps,),
        in_specs=[spec(at) for _, at in flat]
        + [pl.BlockSpec(w.shape, lambda i: (0, 0)) for w in used],
        out_specs=pl.BlockSpec((n_parts, rows // steps, sum(widths)), lambda i: (0, i, 0)),
        out_shape=jax.ShapeDtypeStruct((n_parts, rows, sum(widths)), BF16),
        cost_estimate=cost(1),
        compiler_params=pltpu.CompilerParams(vmem_limit_bytes=32 * MIB),
    )(*[x for x, _ in flat], *used)


def row_sum(mine_ref, theirs_ref):
    n = mine_ref.shape[1] // SIDE
    theirs = jnp.concatenate(
        [theirs_ref[0, (-k % SIDE) * n : (-k % SIDE + 1) * n] for k in range(SIDE)], axis=0
    )
    return mine_ref[0].astype(F32) + theirs.astype(F32)


def hidden_kernel(mine_ref, theirs_ref, out_ref):
    wide = out_ref.shape[0]
    total = row_sum(mine_ref, theirs_ref)
    gate, up = total[:, :wide], total[:, wide:]
    out_ref[...] = (gate * jax.nn.sigmoid(gate) * up).T.astype(BF16)


def grads_kernel(mine_ref, theirs_ref, mine_grad_ref, theirs_grad_ref, out_ref):
    wide = out_ref.shape[0] // 2
    total = row_sum(mine_ref, theirs_ref)
    gate, up = total[:, :wide], total[:, wide:]
    hidden_grad = row_sum(mine_grad_ref, theirs_grad_ref)
    s = jax.nn.sigmoid(gate)
    out_ref[:wide] = (hidden_grad * up * s * (1.0 + gate * (1.0 - s))).T.astype(BF16)
    out_ref[wide:] = (hidden_grad * gate * s).T.astype(BF16)


def activations(kernel, width, *args):
    n_parts, rows, _ = args[0][0].shape

    def spec(columns, block):
        return pl.BlockSpec((1, rows, columns), lambda i: (i, 0, block))

    return pl.pallas_call(
        kernel,
        grid=(n_parts,),
        in_specs=[spec(columns, block) for _, columns, block in args],
        out_specs=pl.BlockSpec((width, rows), lambda i: (0, i)),
        out_shape=jax.ShapeDtypeStruct((width, n_parts * rows), BF16),
        cost_estimate=cost(1),
        compiler_params=pltpu.CompilerParams(vmem_limit_bytes=32 * MIB),
    )(*[x for x, _, _ in args])


def weight_grad_kernel(n_groups, n_parts, before, own, kind, *refs):
    left = refs[:n_groups]
    right = refs[n_groups : n_groups + n_groups * n_parts]
    outs = refs[n_groups + n_groups * n_parts :]
    rows = right[0].shape[0]
    total = None
    if before:
        total, outs = outs[0][...], outs[1:]
    for k in range(n_groups):
        for p in range(n_parts):
            term = plain(left[k][:, p * rows : (p + 1) * rows], right[k * n_parts + p][...])
            total = term if total is None else total + term
    if kind == "sum":
        outs[0][...] = total
    elif kind == "blocks":
        width = outs[0].shape[2]
        for k in range(outs[0].shape[0]):
            outs[0][k] = total[:own, k * width : (k + 1) * width].astype(BF16)
    else:
        half = total.shape[0] // 2
        outs[0][...] = total[:own].astype(BF16)
        outs[1][...] = total[half : half + own].astype(BF16)


def weight_grad(left, right, kind, own, before=None, block=512):
    n_groups, n_parts = len(left), len(right[0])
    flat = [piece for group in right for piece in group]
    rows, features = PIECE, flat[0][0].shape[1]
    hidden = left[0].shape[0]

    def spec(at):
        return pl.BlockSpec((rows, block), lambda i: (at, i))

    in_specs = [pl.BlockSpec(x.shape, lambda i: (0, 0)) for x in left]
    in_specs += [spec(at) for _, at in flat]
    args = [*left, *[x for x, _ in flat]]
    if before is not None:
        in_specs.append(pl.BlockSpec((hidden, block), lambda i: (0, i)))
        args.append(before)
    if kind == "sum":
        out_shape = [jax.ShapeDtypeStruct((hidden, features), F32)]
        out_specs = [pl.BlockSpec((hidden, block), lambda i: (0, i))]
    elif kind == "blocks":
        width = features // N_DEPTH
        out_shape = [jax.ShapeDtypeStruct((N_DEPTH, own, width), BF16)]
        out_specs = [pl.BlockSpec((block // width, own, width), lambda i: (i, 0, 0))]
    else:
        out_shape = [jax.ShapeDtypeStruct((own, features), BF16)] * 2
        out_specs = [pl.BlockSpec((own, block), lambda i: (0, i))] * 2
    return pl.pallas_call(
        lambda *refs: weight_grad_kernel(n_groups, n_parts, before is not None, own, kind, *refs),
        grid=(features // block,),
        in_specs=in_specs,
        out_specs=out_specs,
        out_shape=out_shape,
        cost_estimate=cost(1),
        compiler_params=pltpu.CompilerParams(vmem_limit_bytes=40 * MIB),
    )(*args)


def sums_at(refs, columns):
    return [
        mine[:, columns].astype(F32) + theirs[:, columns].astype(F32)
        for mine, theirs in zip(refs[::2], refs[1::2])
    ]


def mixed_kernel(*refs):
    weight_ref, out_ref, hidden_ref = refs[4:]

    @pl.when(pl.program_id(0) == 0)
    def _():
        for at in range(0, hidden_ref.shape[1], 512):
            columns = slice(at, at + 512)
            gate, up = sums_at(refs[:4], columns)
            hidden_ref[:, columns] = (gate * jax.nn.sigmoid(gate) * up).astype(BF16)

    out_ref[...] = plain(hidden_ref[...], weight_ref[...]).astype(BF16)


def whole(array):
    return pl.BlockSpec(array.shape, lambda i: (0, 0))


def mixed_product(gate_up, weight, block=512):
    width, features = weight.shape
    tokens = gate_up[0].shape[0]
    return pl.pallas_call(
        mixed_kernel,
        grid=(features // block,),
        in_specs=[*map(whole, gate_up), pl.BlockSpec((width, block), lambda i: (0, i))],
        out_specs=pl.BlockSpec((tokens, block), lambda i: (0, i)),
        out_shape=jax.ShapeDtypeStruct((tokens, features), BF16),
        scratch_shapes=[pltpu.VMEM((tokens, width), BF16)],
        cost_estimate=cost(1),
        compiler_params=pltpu.CompilerParams(vmem_limit_bytes=52 * MIB),
    )(*gate_up, weight)


def slice_grads_kernel(*refs):
    refs[6][...], refs[7][...] = gate_up_grads(*sums_at(refs[:6], slice(None)))


def slice_grads(values, block=512):
    tokens, width = values[0].shape
    spec = pl.BlockSpec((tokens, block), lambda i: (0, i))
    return pl.pallas_call(
        slice_grads_kernel,
        grid=(width // block,),
        in_specs=[spec] * 6,
        out_specs=[spec] * 2,
        out_shape=[jax.ShapeDtypeStruct((tokens, width), BF16)] * 2,
        cost_estimate=cost(1),
        compiler_params=pltpu.CompilerParams(vmem_limit_bytes=32 * MIB),
    )(*values)


def input_kernel(grad_gate_ref, grad_up_ref, gate_ref, up_ref, out_ref):
    total = times_transpose(grad_gate_ref[...], gate_ref[...])
    total += times_transpose(grad_up_ref[...], up_ref[...])
    out_ref[...] = total.astype(BF16)


def input_product(grads, gate_weight, up_weight, block=256):
    features, width = gate_weight.shape
    tokens = grads[0].shape[0]
    rows = pl.BlockSpec((block, width), lambda i: (i, 0))
    return pl.pallas_call(
        input_kernel,
        grid=(features // block,),
        in_specs=[*map(whole, grads), rows, rows],
        out_specs=pl.BlockSpec((tokens, block), lambda i: (0, i)),
        out_shape=jax.ShapeDtypeStruct((tokens, features), BF16),
        cost_estimate=cost(1),
        compiler_params=pltpu.CompilerParams(vmem_limit_bytes=52 * MIB),
    )(*grads, gate_weight, up_weight)


def added(terms, start, count):
    total = terms[0][start : start + count].astype(F32)
    for term in terms[1:]:
        total = total + term[start : start + count].astype(F32)
    return total.astype(BF16)


def per_device(tokens, gate_weight, up_weight, down_weight, cotangent):
    core = lax.axis_index("row").astype(jnp.int32).reshape(1)
    depth = lax.axis_index("depth")
    rows = tokens.shape[0]
    hidden_width = gate_weight.shape[1]
    own = hidden_width // N_DEPTH
    wide = -(-own // 128) * 128

    n = rows // 3
    thirds = [[(0, p * n, n), (1, p * n, n)] for p in range(3)]
    mine, zs, ys = regroup(
        core, [tokens, cotangent], [thirds[0] + thirds[1] + thirds[2], thirds[1], thirds[2]]
    )
    xs = [mine] + [shift(mine, "x", s) for s in (1, 2, -1)]
    zs, ys = ring(zs, "z"), ring(ys, "y")

    def joined(pieces, half):
        orders = ((0, 1, 2, 3), (0, 3, 2, 1))
        plans = [[[(i, c * half, half) for c in range(2) for i in order]] for order in orders]
        return regroup(core, pieces, *plans)[0]

    def stacked(pieces, half):
        return regroup(core, pieces, [[(i, c * half, half) for c in range(2) for i in range(4)]])[0]

    panel_plan = [[(i, 2 * n * p + n * c, n) for i in range(4) for p in range(3)] for c in range(2)]
    first_plan = [(i, n * c, n) for c in range(2) for i in range(4)]
    panel, grad_panel, r0 = regroup(core, xs, [*panel_plan, first_plan])
    t0, q0 = joined(zs, n), joined(ys, n)
    r1, t1, q1 = hop(r0, "y"), hop(t0, "x"), hop(q0, "z")

    def own_columns(weight):
        cut = lax.dynamic_slice_in_dim(weight, depth * own, own, axis=1)
        return jnp.pad(cut, ((0, 0), (0, wide - own)))

    own_gate_up = jnp.concatenate([own_columns(gate_weight), own_columns(up_weight)], axis=1)
    own_down = jnp.pad(
        lax.dynamic_slice_in_dim(down_weight, depth * own, own, axis=0), ((0, wide - own), (0, 0))
    )

    (panel_,) = tie((panel,), r0, own_gate_up, own_down)
    gate_part = plain(panel_, gate_weight).astype(BF16)

    (panel_,) = tie((panel,), gate_part, r1, t1, q1)
    (r1_, t1_, q1_) = tie((r1, t1, q1), gate_part)
    r2, t2, q2 = hop(r1_, "y"), hop(t1_, "x"), hop(q1_, "z")
    up_part = plain(panel_, up_weight).astype(BF16)
    gate_theirs = swap(gate_part)

    (grad_panel,) = tie((grad_panel,), up_part, r2, t2, q2, gate_theirs)
    (r2_, t2_, q2_) = tie((r2, t2, q2), up_part)
    r3, t3, q3 = hop(r2_, "y"), hop(t2_, "x"), hop(q2_, "z")
    up_theirs = swap(up_part)
    grad_part = times_transpose(grad_panel, down_weight).astype(BF16)

    r0, r1, r2, r3 = tie((r0, r1, r2, r3), grad_part, up_theirs)
    t0, t1, t2, t3 = tie((t0, t1, t2, t3), grad_part)
    q0, q1, q2, q3 = tie((q0, q1, q2, q3), grad_part)
    grad_theirs = swap(grad_part)
    axes = ("z", "y", "x")

    def hops(pieces, *deps):
        return [hop(*tie((x,), *deps), axis) for x, axis in zip(pieces, axes)]

    both = [[stacked(x, 4 * n) for x in ((r0, r1, r2, r3), (t0, t1, t2, t3), (q0, q1, q2, q3))]]
    both.append(hops(both[0]))
    toks, cots = [[(x, 0) for x in both[0]]], [[(x, 1) for x in both[0]]]
    (gate_part_,) = tie((gate_part,), *both[0])
    gate_up = (gate_theirs, up_part, up_theirs)
    mixed_part = mixed_product((gate_part_, *gate_up), down_weight)
    (own_down_,) = tie((own_down,), mixed_part)
    u0 = own_partials([toks[0], cots[0]], (own_gate_up, own_down_), (0, 1))
    v0 = swap(u0)
    (gate_part_,) = tie((gate_part,), u0)
    grads = slice_grads((gate_part_, *gate_up, grad_part, grad_theirs))

    both.append(hops(both[1], *grads))
    toks.append([(x, 0) for x in both[1]])
    cots.append([(x, 1) for x in both[1]])
    input_part = input_product(tie(tuple(grads), *both[1]), gate_weight, up_weight)
    (own_down_,) = tie((own_down,), input_part)
    u1 = own_partials([toks[1], cots[1]], (own_gate_up, own_down_), (0, 1))
    v1 = swap(u1)
    back_plan = [[(p, back * rows, rows) for p in range(2)] for back in range(N_COL)]
    sums = regroup(core, [mixed_part, input_part], back_plan)

    both.append(hops(both[2], u1, v0, v1, *sums))
    toks.append([(x, 0) for x in both[2]])
    cots.append([(x, 1) for x in both[2]])
    (own_down_,) = tie((own_down,), u1, *both[2])
    u2 = own_partials([toks[2], cots[2]], (own_gate_up, own_down_), (0, 1))
    v2 = swap(u2)

    def hidden_of(mine, theirs):
        return activations(hidden_kernel, wide, *[(x, 2 * wide, 0) for x in (mine, theirs)])

    def grads_of(mine, theirs, *grads):
        pre = [(x, 2 * wide, 0) for x in (mine, theirs)]
        return activations(grads_kernel, 2 * wide, *pre, *[(x, wide, at) for x, at in grads])

    (u0,) = tie((u0,), u2)
    h0 = hidden_of(u0, v0)
    d0 = grads_of(u0, v0, (u0, 2), (v0, 2))
    (u2,) = tie((u2,), d0)
    h2 = hidden_of(u2, v2)
    d2 = grads_of(u2, v2, (u2, 2), (v2, 2))
    (h2,) = tie((h2,), d2)
    (down_early,) = weight_grad([h0, h2], [cots[0], cots[2]], "sum", own)
    (d2,) = tie((d2,), down_early)
    (grads_early,) = weight_grad([d0, d2], [toks[0], toks[2]], "sum", own)

    toks.append([(x, 0) for x in both[3]])
    cots.append([(x, 1) for x in both[3]])
    (own_gate_up_,) = tie((own_gate_up,), grads_early, *both[3])
    u3 = own_partials([toks[3]], (own_gate_up_, None), (0,))
    v3 = swap(u3)
    h3 = hidden_of(u3, v1)
    (u1,) = tie((u1,), h3)
    h1 = hidden_of(u1, v3)
    (down_blocks,) = weight_grad([h1, h3], [cots[1], cots[3]], "blocks", own, before=down_early)
    down_grad = lax.all_to_all(down_blocks, "depth", split_axis=0, concat_axis=0, tiled=True)

    (own_down_,) = tie((own_down,), h3)
    w3 = own_partials([cots[3]], (None, own_down_), (1,))
    z3 = swap(w3)
    (u3,) = tie((u3,), down_blocks)
    d3 = grads_of(u3, v1, (w3, 0), (v1, 2))
    sums = tie(tuple(sums), u3)
    sums = [sums[0]] + [shift(sums[back], "x", -back) for back in range(1, N_COL)]
    d1 = grads_of(u1, v3, (u1, 2), (z3, 0))
    gate_grad, up_grad = weight_grad(
        [d1, d3], [toks[1], toks[3]], "pair", own, before=grads_early
    )
    down_grad = down_grad.reshape(hidden_width, -1)
    sums = tie(tuple(sums), gate_grad)
    mixed, input_grad = added(sums, 0, rows), added(sums, rows, rows)
    return mixed, input_grad, gate_grad.T, up_grad.T, down_grad


def solution(mesh):
    placed = (
        P(("col", "depth"), "row"),
        P("row", "col"),
        P("row", "col"),
        P("col", "row"),
        P(("col", "depth"), "row"),
    )
    return jax.shard_map(
        per_device,
        mesh=mesh,
        in_specs=placed,
        out_specs=(
            P(("col", "depth"), "row"),
            P(("col", "depth"), "row"),
            P("row", ("col", "depth")),
            P("row", ("col", "depth")),
            P("col", ("row", "depth")),
        ),
        check_vma=False,
    )
```

```python
import functools

import jax
import jax.numpy as jnp
from jax import lax
from jax.experimental import pallas as pl
from jax.experimental.pallas import tpu as pltpu
from jax.sharding import PartitionSpec as P

N_COL = 4
N_DEPTH = 16
SIDE = 4
PIECE = 256
BF16 = jnp.bfloat16
F32 = jnp.float32
LAST = (((1,), (1,)), ((), ()))
MIB = 1024 * 1024


def shifted(axis, index, step):
    if axis == "x":
        return (index + step) % N_COL
    z, y = divmod(index, SIDE)
    if axis == "y":
        return z * SIDE + (y + step) % SIDE
    return ((z + step) % SIDE) * SIDE + y


def extent(axis):
    return N_COL if axis == "x" else N_DEPTH


def mesh_axis(axis):
    return "col" if axis == "x" else "depth"


def hop(array, axis):
    n = extent(axis)
    pairs = [
        (core * n + i, core * n + shifted(axis, i, 1 - 2 * core))
        for core in range(2)
        for i in range(n)
    ]
    return lax.ppermute(array, ("row", mesh_axis(axis)), pairs)


def shift(array, axis, step):
    pairs = [(i, shifted(axis, i, step)) for i in range(extent(axis))]
    return lax.ppermute(array, mesh_axis(axis), pairs)


def swap(array):
    return lax.ppermute(array, "row", [(0, 1), (1, 0)])


def ring(array, axis):
    pieces = [array]
    for _ in range(SIDE - 1):
        pieces.append(hop(pieces[-1], axis))
    return pieces


def tie(values, *deps):
    return lax.optimization_barrier((*values, *deps))[: len(values)]


def regroup_kernel(n_in, plans, core_ref, *refs):
    def copy(plan):
        for out_ref, rows in zip(refs[n_in:], plan):
            at = 0
            for source, start, count in rows:
                out_ref[at : at + count] = refs[source][start : start + count]
                at += count

    if len(plans) == 1:
        copy(plans[0])
    else:
        for c, plan in enumerate(plans):
            pl.when(core_ref[0] == c)(functools.partial(copy, plan))


def regroup(core, arrays, *plans):
    features = arrays[0].shape[1]
    counts = [sum(count for _, _, count in rows) for rows in plans[0]]
    return pl.pallas_call(
        lambda *refs: regroup_kernel(len(arrays), plans, *refs),
        in_specs=[pl.BlockSpec(memory_space=pltpu.SMEM)]
        + [pl.BlockSpec(memory_space=pltpu.VMEM)] * len(arrays),
        out_shape=[jax.ShapeDtypeStruct((n, features), BF16) for n in counts],
        cost_estimate=cost(1),
        compiler_params=pltpu.CompilerParams(vmem_limit_bytes=16 * MIB),
    )(core, *arrays)


def times_transpose(left, right):
    return lax.dot_general(left, right, LAST, preferred_element_type=F32)


def plain(left, right):
    return jnp.dot(left, right, preferred_element_type=F32)


def gate_up_grads(gate, up, hidden_grad):
    s = jax.nn.sigmoid(gate)
    grad_up = (hidden_grad * gate * s).astype(BF16)
    grad_gate = (hidden_grad * up * s * (1.0 + gate * (1.0 - s))).astype(BF16)
    return grad_gate, grad_up


def cost(megabytes):
    return pl.CostEstimate(flops=0, bytes_accessed=int(megabytes * 1e6), transcendentals=0)


def own_partials_kernel(n_parts, sides, *refs):
    weights, out_ref = refs[len(sides) * n_parts : -1], refs[-1]
    rows = out_ref.shape[1]
    at = 0
    for s, (side, weight_ref) in enumerate(zip(sides, weights)):
        left = jnp.concatenate([x[...] for x in refs[s * n_parts : (s + 1) * n_parts]], axis=0)
        product = (times_transpose if side else plain)(left, weight_ref[...]).astype(BF16)
        width = product.shape[1]
        for p in range(n_parts):
            out_ref[p, :, at : at + width] = product[p * rows : (p + 1) * rows]
        at += width


def own_partials(pieces, weights, sides, steps=2):
    n_parts = len(pieces[0])
    flat = [x for side in pieces for x in side]
    rows, features = PIECE, flat[0][0].shape[1]
    used = [weights[side] for side in sides]
    widths = [w.shape[0] if side else w.shape[1] for side, w in zip(sides, used)]

    def spec(at):
        return pl.BlockSpec((rows // steps, features), lambda i: (at * steps + i, 0))

    return pl.pallas_call(
        lambda *refs: own_partials_kernel(n_parts, sides, *refs),
        grid=(steps,),
        in_specs=[spec(at) for _, at in flat]
        + [pl.BlockSpec(w.shape, lambda i: (0, 0)) for w in used],
        out_specs=pl.BlockSpec((n_parts, rows // steps, sum(widths)), lambda i: (0, i, 0)),
        out_shape=jax.ShapeDtypeStruct((n_parts, rows, sum(widths)), BF16),
        cost_estimate=cost(1),
        compiler_params=pltpu.CompilerParams(vmem_limit_bytes=32 * MIB),
    )(*[x for x, _ in flat], *used)


def row_sum(mine_ref, theirs_ref):
    n = mine_ref.shape[1] // SIDE
    theirs = jnp.concatenate(
        [theirs_ref[0, (-k % SIDE) * n : (-k % SIDE + 1) * n] for k in range(SIDE)], axis=0
    )
    return mine_ref[0].astype(F32) + theirs.astype(F32)


def hidden_kernel(mine_ref, theirs_ref, out_ref):
    wide = out_ref.shape[0]
    total = row_sum(mine_ref, theirs_ref)
    gate, up = total[:, :wide], total[:, wide:]
    out_ref[...] = (gate * jax.nn.sigmoid(gate) * up).T.astype(BF16)


def grads_kernel(mine_ref, theirs_ref, mine_grad_ref, theirs_grad_ref, out_ref):
    wide = out_ref.shape[0] // 2
    total = row_sum(mine_ref, theirs_ref)
    gate, up = total[:, :wide], total[:, wide:]
    hidden_grad = row_sum(mine_grad_ref, theirs_grad_ref)
    s = jax.nn.sigmoid(gate)
    out_ref[:wide] = (hidden_grad * up * s * (1.0 + gate * (1.0 - s))).T.astype(BF16)
    out_ref[wide:] = (hidden_grad * gate * s).T.astype(BF16)


def activations(kernel, width, *args):
    n_parts, rows, _ = args[0][0].shape

    def spec(columns, block):
        return pl.BlockSpec((1, rows, columns), lambda i: (i, 0, block))

    return pl.pallas_call(
        kernel,
        grid=(n_parts,),
        in_specs=[spec(columns, block) for _, columns, block in args],
        out_specs=pl.BlockSpec((width, rows), lambda i: (0, i)),
        out_shape=jax.ShapeDtypeStruct((width, n_parts * rows), BF16),
        cost_estimate=cost(1),
        compiler_params=pltpu.CompilerParams(vmem_limit_bytes=32 * MIB),
    )(*[x for x, _, _ in args])


def weight_grad_kernel(n_groups, n_parts, before, own, kind, *refs):
    left = refs[:n_groups]
    right = refs[n_groups : n_groups + n_groups * n_parts]
    outs = refs[n_groups + n_groups * n_parts :]
    rows = right[0].shape[0]
    total = None
    if before:
        total, outs = outs[0][...], outs[1:]
    for k in range(n_groups):
        for p in range(n_parts):
            term = plain(left[k][:, p * rows : (p + 1) * rows], right[k * n_parts + p][...])
            total = term if total is None else total + term
    if kind == "sum":
        outs[0][...] = total
    elif kind == "blocks":
        width = outs[0].shape[2]
        for k in range(outs[0].shape[0]):
            outs[0][k] = total[:own, k * width : (k + 1) * width].astype(BF16)
    else:
        half = total.shape[0] // 2
        outs[0][...] = total[:own].astype(BF16)
        outs[1][...] = total[half : half + own].astype(BF16)


def weight_grad(left, right, kind, own, before=None, block=512):
    n_groups, n_parts = len(left), len(right[0])
    flat = [piece for group in right for piece in group]
    rows, features = PIECE, flat[0][0].shape[1]
    hidden = left[0].shape[0]

    def spec(at):
        return pl.BlockSpec((rows, block), lambda i: (at, i))

    in_specs = [pl.BlockSpec(x.shape, lambda i: (0, 0)) for x in left]
    in_specs += [spec(at) for _, at in flat]
    args = [*left, *[x for x, _ in flat]]
    if before is not None:
        in_specs.append(pl.BlockSpec((hidden, block), lambda i: (0, i)))
        args.append(before)
    if kind == "sum":
        out_shape = [jax.ShapeDtypeStruct((hidden, features), F32)]
        out_specs = [pl.BlockSpec((hidden, block), lambda i: (0, i))]
    elif kind == "blocks":
        width = features // N_DEPTH
        out_shape = [jax.ShapeDtypeStruct((N_DEPTH, own, width), BF16)]
        out_specs = [pl.BlockSpec((block // width, own, width), lambda i: (i, 0, 0))]
    else:
        out_shape = [jax.ShapeDtypeStruct((own, features), BF16)] * 2
        out_specs = [pl.BlockSpec((own, block), lambda i: (0, i))] * 2
    return pl.pallas_call(
        lambda *refs: weight_grad_kernel(n_groups, n_parts, before is not None, own, kind, *refs),
        grid=(features // block,),
        in_specs=in_specs,
        out_specs=out_specs,
        out_shape=out_shape,
        cost_estimate=cost(1),
        compiler_params=pltpu.CompilerParams(vmem_limit_bytes=40 * MIB),
    )(*args)


def transposed_kernel(left_ref, weight_ref, out_ref):
    out_ref[...] = times_transpose(left_ref[...], weight_ref[...]).astype(BF16)


def transposed_product(left, weight, block=896):
    width, features = weight.shape
    tokens = left.shape[0]
    return pl.pallas_call(
        transposed_kernel,
        grid=(width // block,),
        in_specs=[whole(left), pl.BlockSpec((block, features), lambda i: (i, 0))],
        out_specs=pl.BlockSpec((tokens, block), lambda i: (0, i)),
        out_shape=jax.ShapeDtypeStruct((tokens, width), BF16),
        cost_estimate=pl.CostEstimate(
            flops=8 * tokens * width * features,
            bytes_accessed=8 * width * features,
            transcendentals=0,
        ),
        compiler_params=pltpu.CompilerParams(vmem_limit_bytes=24 * MIB),
    )(left, weight)


def sums_at(refs, columns):
    return [
        mine[:, columns].astype(F32) + theirs[:, columns].astype(F32)
        for mine, theirs in zip(refs[::2], refs[1::2])
    ]


def mixed_kernel(*refs):
    weight_ref, out_ref, hidden_ref = refs[4:]

    @pl.when(pl.program_id(0) == 0)
    def _():
        for at in range(0, hidden_ref.shape[1], 512):
            columns = slice(at, at + 512)
            gate, up = sums_at(refs[:4], columns)
            hidden_ref[:, columns] = (gate * jax.nn.sigmoid(gate) * up).astype(BF16)

    out_ref[...] = plain(hidden_ref[...], weight_ref[...]).astype(BF16)


def whole(array):
    return pl.BlockSpec(array.shape, lambda i: (0, 0))


def mixed_product(gate_up, weight, block=512):
    width, features = weight.shape
    tokens = gate_up[0].shape[0]
    return pl.pallas_call(
        mixed_kernel,
        grid=(features // block,),
        in_specs=[*map(whole, gate_up), pl.BlockSpec((width, block), lambda i: (0, i))],
        out_specs=pl.BlockSpec((tokens, block), lambda i: (0, i)),
        out_shape=jax.ShapeDtypeStruct((tokens, features), BF16),
        scratch_shapes=[pltpu.VMEM((tokens, width), BF16)],
        cost_estimate=cost(1),
        compiler_params=pltpu.CompilerParams(vmem_limit_bytes=52 * MIB),
    )(*gate_up, weight)


def slice_grads_kernel(*refs):
    refs[6][...], refs[7][...] = gate_up_grads(*sums_at(refs[:6], slice(None)))


def slice_grads(values, block=512):
    tokens, width = values[0].shape
    spec = pl.BlockSpec((tokens, block), lambda i: (0, i))
    return pl.pallas_call(
        slice_grads_kernel,
        grid=(width // block,),
        in_specs=[spec] * 6,
        out_specs=[spec] * 2,
        out_shape=[jax.ShapeDtypeStruct((tokens, width), BF16)] * 2,
        cost_estimate=cost(1),
        compiler_params=pltpu.CompilerParams(vmem_limit_bytes=32 * MIB),
    )(*values)


def input_kernel(grad_gate_ref, grad_up_ref, gate_ref, up_ref, out_ref):
    total = times_transpose(grad_gate_ref[...], gate_ref[...])
    total += times_transpose(grad_up_ref[...], up_ref[...])
    out_ref[...] = total.astype(BF16)


def input_product(grads, gate_weight, up_weight, block=256):
    features, width = gate_weight.shape
    tokens = grads[0].shape[0]
    rows = pl.BlockSpec((block, width), lambda i: (i, 0))
    return pl.pallas_call(
        input_kernel,
        grid=(features // block,),
        in_specs=[*map(whole, grads), rows, rows],
        out_specs=pl.BlockSpec((tokens, block), lambda i: (0, i)),
        out_shape=jax.ShapeDtypeStruct((tokens, features), BF16),
        cost_estimate=cost(1),
        compiler_params=pltpu.CompilerParams(vmem_limit_bytes=52 * MIB),
    )(*grads, gate_weight, up_weight)


def added(terms, start, count):
    total = terms[0][start : start + count].astype(F32)
    for term in terms[1:]:
        total = total + term[start : start + count].astype(F32)
    return total.astype(BF16)


def per_device(tokens, gate_weight, up_weight, down_weight, cotangent):
    core = lax.axis_index("row").astype(jnp.int32).reshape(1)
    depth = lax.axis_index("depth")
    rows = tokens.shape[0]
    hidden_width = gate_weight.shape[1]
    own = hidden_width // N_DEPTH
    wide = -(-own // 128) * 128

    n = rows // 3
    thirds = [[(0, p * n, n), (1, p * n, n)] for p in range(3)]
    mine, zs, ys = regroup(
        core, [tokens, cotangent], [thirds[0] + thirds[1] + thirds[2], thirds[1], thirds[2]]
    )
    xs = [mine] + [shift(mine, "x", s) for s in (1, 2, -1)]
    zs, ys = ring(zs, "z"), ring(ys, "y")

    def joined(pieces, half):
        orders = ((0, 1, 2, 3), (0, 3, 2, 1))
        plans = [[[(i, c * half, half) for c in range(2) for i in order]] for order in orders]
        return regroup(core, pieces, *plans)[0]

    def stacked(pieces, half):
        return regroup(core, pieces, [[(i, c * half, half) for c in range(2) for i in range(4)]])[0]

    panel_plan = [[(i, 2 * n * p + n * c, n) for i in range(4) for p in range(3)] for c in range(2)]
    first_plan = [(i, n * c, n) for c in range(2) for i in range(4)]
    panel, grad_panel, r0 = regroup(core, xs, [*panel_plan, first_plan])
    t0, q0 = joined(zs, n), joined(ys, n)
    r1, t1, q1 = hop(r0, "y"), hop(t0, "x"), hop(q0, "z")

    def own_columns(weight):
        cut = lax.dynamic_slice_in_dim(weight, depth * own, own, axis=1)
        return jnp.pad(cut, ((0, 0), (0, wide - own)))

    own_gate_up = jnp.concatenate([own_columns(gate_weight), own_columns(up_weight)], axis=1)
    own_down = jnp.pad(
        lax.dynamic_slice_in_dim(down_weight, depth * own, own, axis=0), ((0, wide - own), (0, 0))
    )

    (panel_,) = tie((panel,), r0, own_gate_up, own_down)
    gate_part = plain(panel_, gate_weight).astype(BF16)

    (panel_,) = tie((panel,), gate_part, r1, t1, q1)
    (r1_, t1_, q1_) = tie((r1, t1, q1), gate_part)
    r2, t2, q2 = hop(r1_, "y"), hop(t1_, "x"), hop(q1_, "z")
    up_part = plain(panel_, up_weight).astype(BF16)
    gate_theirs = swap(gate_part)

    (grad_panel,) = tie((grad_panel,), up_part, r2, t2, q2, gate_theirs)
    (r2_, t2_, q2_) = tie((r2, t2, q2), up_part)
    r3, t3, q3 = hop(r2_, "y"), hop(t2_, "x"), hop(q2_, "z")
    up_theirs = swap(up_part)
    grad_part = transposed_product(grad_panel, down_weight)

    r0, r1, r2, r3 = tie((r0, r1, r2, r3), grad_part, up_theirs)
    t0, t1, t2, t3 = tie((t0, t1, t2, t3), grad_part)
    q0, q1, q2, q3 = tie((q0, q1, q2, q3), grad_part)
    grad_theirs = swap(grad_part)
    axes = ("z", "y", "x")

    def hops(pieces, *deps):
        return [hop(*tie((x,), *deps), axis) for x, axis in zip(pieces, axes)]

    both = [[stacked(x, 4 * n) for x in ((r0, r1, r2, r3), (t0, t1, t2, t3), (q0, q1, q2, q3))]]
    both.append(hops(both[0]))
    toks, cots = [[(x, 0) for x in both[0]]], [[(x, 1) for x in both[0]]]
    (gate_part_,) = tie((gate_part,), *both[0])
    gate_up = (gate_theirs, up_part, up_theirs)
    mixed_part = mixed_product((gate_part_, *gate_up), down_weight)
    (own_down_,) = tie((own_down,), mixed_part)
    u0 = own_partials([toks[0], cots[0]], (own_gate_up, own_down_), (0, 1))
    v0 = swap(u0)
    (gate_part_,) = tie((gate_part,), u0)
    grads = slice_grads((gate_part_, *gate_up, grad_part, grad_theirs))

    both.append(hops(both[1], *grads))
    toks.append([(x, 0) for x in both[1]])
    cots.append([(x, 1) for x in both[1]])
    input_part = input_product(tie(tuple(grads), *both[1]), gate_weight, up_weight)
    (own_down_,) = tie((own_down,), input_part)
    u1 = own_partials([toks[1], cots[1]], (own_gate_up, own_down_), (0, 1))
    v1 = swap(u1)
    back_plan = [[(p, back * rows, rows) for p in range(2)] for back in range(N_COL)]
    sums = regroup(core, [mixed_part, input_part], back_plan)

    both.append(hops(both[2], u1, v0, v1, *sums))
    toks.append([(x, 0) for x in both[2]])
    cots.append([(x, 1) for x in both[2]])
    (own_down_,) = tie((own_down,), u1, *both[2])
    u2 = own_partials([toks[2], cots[2]], (own_gate_up, own_down_), (0, 1))
    v2 = swap(u2)

    def hidden_of(mine, theirs):
        return activations(hidden_kernel, wide, *[(x, 2 * wide, 0) for x in (mine, theirs)])

    def grads_of(mine, theirs, *grads):
        pre = [(x, 2 * wide, 0) for x in (mine, theirs)]
        return activations(grads_kernel, 2 * wide, *pre, *[(x, wide, at) for x, at in grads])

    (u0,) = tie((u0,), u2)
    h0 = hidden_of(u0, v0)
    d0 = grads_of(u0, v0, (u0, 2), (v0, 2))
    (u2,) = tie((u2,), d0)
    h2 = hidden_of(u2, v2)
    d2 = grads_of(u2, v2, (u2, 2), (v2, 2))
    (h2,) = tie((h2,), d2)
    (down_early,) = weight_grad([h0, h2], [cots[0], cots[2]], "sum", own)
    (d2,) = tie((d2,), down_early)
    (grads_early,) = weight_grad([d0, d2], [toks[0], toks[2]], "sum", own)

    toks.append([(x, 0) for x in both[3]])
    cots.append([(x, 1) for x in both[3]])
    (own_gate_up_,) = tie((own_gate_up,), grads_early, *both[3])
    u3 = own_partials([toks[3]], (own_gate_up_, None), (0,))
    v3 = swap(u3)
    h3 = hidden_of(u3, v1)
    (u1,) = tie((u1,), h3)
    h1 = hidden_of(u1, v3)
    (down_blocks,) = weight_grad([h1, h3], [cots[1], cots[3]], "blocks", own, before=down_early)
    down_grad = lax.all_to_all(down_blocks, "depth", split_axis=0, concat_axis=0, tiled=True)

    (own_down_,) = tie((own_down,), h3)
    w3 = own_partials([cots[3]], (None, own_down_), (1,))
    z3 = swap(w3)
    (u3,) = tie((u3,), down_blocks)
    d3 = grads_of(u3, v1, (w3, 0), (v1, 2))
    sums = tie(tuple(sums), u3)
    sums = [sums[0]] + [shift(sums[back], "x", -back) for back in range(1, N_COL)]
    d1 = grads_of(u1, v3, (u1, 2), (z3, 0))
    gate_grad, up_grad = weight_grad(
        [d1, d3], [toks[1], toks[3]], "pair", own, before=grads_early
    )
    down_grad = down_grad.reshape(hidden_width, -1)
    sums = tie(tuple(sums), gate_grad)
    mixed, input_grad = added(sums, 0, rows), added(sums, rows, rows)
    return mixed, input_grad, gate_grad.T, up_grad.T, down_grad


def solution(mesh):
    placed = (
        P(("col", "depth"), "row"),
        P("row", "col"),
        P("row", "col"),
        P("col", "row"),
        P(("col", "depth"), "row"),
    )
    return jax.shard_map(
        per_device,
        mesh=mesh,
        in_specs=placed,
        out_specs=(
            P(("col", "depth"), "row"),
            P(("col", "depth"), "row"),
            P("row", ("col", "depth")),
            P("row", ("col", "depth")),
            P("col", ("row", "depth")),
        ),
        check_vma=False,
    )
```

```python
import functools

import jax
import jax.numpy as jnp
from jax import lax
from jax.experimental import pallas as pl
from jax.experimental.pallas import tpu as pltpu
from jax.sharding import PartitionSpec as P

N_COL = 4
N_DEPTH = 16
SIDE = 4
PIECE = 256
BF16 = jnp.bfloat16
F32 = jnp.float32
LAST = (((1,), (1,)), ((), ()))
MIB = 1024 * 1024


def shifted(axis, index, step):
    if axis == "x":
        return (index + step) % N_COL
    z, y = divmod(index, SIDE)
    if axis == "y":
        return z * SIDE + (y + step) % SIDE
    return ((z + step) % SIDE) * SIDE + y


def extent(axis):
    return N_COL if axis == "x" else N_DEPTH


def mesh_axis(axis):
    return "col" if axis == "x" else "depth"


def hop(array, axis):
    n = extent(axis)
    pairs = [
        (core * n + i, core * n + shifted(axis, i, 1 - 2 * core))
        for core in range(2)
        for i in range(n)
    ]
    return lax.ppermute(array, ("row", mesh_axis(axis)), pairs)


def shift(array, axis, step):
    pairs = [(i, shifted(axis, i, step)) for i in range(extent(axis))]
    return lax.ppermute(array, mesh_axis(axis), pairs)


def swap(array):
    return lax.ppermute(array, "row", [(0, 1), (1, 0)])


def ring(array, axis):
    pieces = [array]
    for _ in range(SIDE - 1):
        pieces.append(hop(pieces[-1], axis))
    return pieces


def tie(values, *deps):
    return lax.optimization_barrier((*values, *deps))[: len(values)]


def regroup_kernel(n_in, plans, core_ref, *refs):
    def copy(plan):
        for out_ref, rows in zip(refs[n_in:], plan):
            at = 0
            for source, start, count in rows:
                out_ref[at : at + count] = refs[source][start : start + count]
                at += count

    if len(plans) == 1:
        copy(plans[0])
    else:
        for c, plan in enumerate(plans):
            pl.when(core_ref[0] == c)(functools.partial(copy, plan))


def regroup(core, arrays, *plans):
    features = arrays[0].shape[1]
    counts = [sum(count for _, _, count in rows) for rows in plans[0]]
    return pl.pallas_call(
        lambda *refs: regroup_kernel(len(arrays), plans, *refs),
        in_specs=[pl.BlockSpec(memory_space=pltpu.SMEM)]
        + [pl.BlockSpec(memory_space=pltpu.VMEM)] * len(arrays),
        out_shape=[jax.ShapeDtypeStruct((n, features), BF16) for n in counts],
        cost_estimate=cost(1),
        compiler_params=pltpu.CompilerParams(vmem_limit_bytes=16 * MIB),
    )(core, *arrays)


def times_transpose(left, right):
    return lax.dot_general(left, right, LAST, preferred_element_type=F32)


def plain(left, right):
    return jnp.dot(left, right, preferred_element_type=F32)


def gate_up_grads(gate, up, hidden_grad):
    s = jax.nn.sigmoid(gate)
    grad_up = (hidden_grad * gate * s).astype(BF16)
    grad_gate = (hidden_grad * up * s * (1.0 + gate * (1.0 - s))).astype(BF16)
    return grad_gate, grad_up


def cost(megabytes):
    return pl.CostEstimate(flops=0, bytes_accessed=int(megabytes * 1e6), transcendentals=0)


def own_partials_kernel(n_parts, sides, *refs):
    weights, out_ref = refs[len(sides) * n_parts : -1], refs[-1]
    rows = out_ref.shape[1]
    at = 0
    for s, (side, weight_ref) in enumerate(zip(sides, weights)):
        left = jnp.concatenate([x[...] for x in refs[s * n_parts : (s + 1) * n_parts]], axis=0)
        product = (times_transpose if side else plain)(left, weight_ref[...]).astype(BF16)
        width = product.shape[1]
        for p in range(n_parts):
            out_ref[p, :, at : at + width] = product[p * rows : (p + 1) * rows]
        at += width


def own_partials(pieces, weights, sides, steps=2):
    n_parts = len(pieces[0])
    flat = [x for side in pieces for x in side]
    rows, features = PIECE, flat[0][0].shape[1]
    used = [weights[side] for side in sides]
    widths = [w.shape[0] if side else w.shape[1] for side, w in zip(sides, used)]

    def spec(at):
        return pl.BlockSpec((rows // steps, features), lambda i: (at * steps + i, 0))

    return pl.pallas_call(
        lambda *refs: own_partials_kernel(n_parts, sides, *refs),
        grid=(steps,),
        in_specs=[spec(at) for _, at in flat]
        + [pl.BlockSpec(w.shape, lambda i: (0, 0)) for w in used],
        out_specs=pl.BlockSpec((n_parts, rows // steps, sum(widths)), lambda i: (0, i, 0)),
        out_shape=jax.ShapeDtypeStruct((n_parts, rows, sum(widths)), BF16),
        cost_estimate=cost(1),
        compiler_params=pltpu.CompilerParams(vmem_limit_bytes=32 * MIB),
    )(*[x for x, _ in flat], *used)


def row_sum(mine_ref, theirs_ref):
    n = mine_ref.shape[1] // SIDE
    theirs = jnp.concatenate(
        [theirs_ref[0, (-k % SIDE) * n : (-k % SIDE + 1) * n] for k in range(SIDE)], axis=0
    )
    return mine_ref[0].astype(F32) + theirs.astype(F32)


def hidden_kernel(mine_ref, theirs_ref, out_ref):
    wide = out_ref.shape[0]
    total = row_sum(mine_ref, theirs_ref)
    gate, up = total[:, :wide], total[:, wide:]
    out_ref[...] = (gate * jax.nn.sigmoid(gate) * up).T.astype(BF16)


def grads_kernel(mine_ref, theirs_ref, mine_grad_ref, theirs_grad_ref, out_ref):
    wide = out_ref.shape[0] // 2
    total = row_sum(mine_ref, theirs_ref)
    gate, up = total[:, :wide], total[:, wide:]
    hidden_grad = row_sum(mine_grad_ref, theirs_grad_ref)
    s = jax.nn.sigmoid(gate)
    out_ref[:wide] = (hidden_grad * up * s * (1.0 + gate * (1.0 - s))).T.astype(BF16)
    out_ref[wide:] = (hidden_grad * gate * s).T.astype(BF16)


def activations(kernel, width, *args):
    n_parts, rows, _ = args[0][0].shape

    def spec(columns, block):
        return pl.BlockSpec((1, rows, columns), lambda i: (i, 0, block))

    return pl.pallas_call(
        kernel,
        grid=(n_parts,),
        in_specs=[spec(columns, block) for _, columns, block in args],
        out_specs=pl.BlockSpec((width, rows), lambda i: (0, i)),
        out_shape=jax.ShapeDtypeStruct((width, n_parts * rows), BF16),
        cost_estimate=cost(1),
        compiler_params=pltpu.CompilerParams(vmem_limit_bytes=32 * MIB),
    )(*[x for x, _, _ in args])


def weight_grad_kernel(n_groups, n_parts, before, own, kind, *refs):
    left = refs[:n_groups]
    right = refs[n_groups : n_groups + n_groups * n_parts]
    outs = refs[n_groups + n_groups * n_parts :]
    rows = right[0].shape[0]
    total = None
    if before:
        total, outs = outs[0][...], outs[1:]
    for k in range(n_groups):
        for p in range(n_parts):
            term = plain(left[k][:, p * rows : (p + 1) * rows], right[k * n_parts + p][...])
            total = term if total is None else total + term
    if kind == "sum":
        outs[0][...] = total
    elif kind == "blocks":
        width = outs[0].shape[2]
        for k in range(outs[0].shape[0]):
            outs[0][k] = total[:own, k * width : (k + 1) * width].astype(BF16)
    else:
        half = total.shape[0] // 2
        outs[0][...] = total[:own].astype(BF16)
        outs[1][...] = total[half : half + own].astype(BF16)


def weight_grad(left, right, kind, own, before=None, block=512):
    n_groups, n_parts = len(left), len(right[0])
    flat = [piece for group in right for piece in group]
    rows, features = PIECE, flat[0][0].shape[1]
    hidden = left[0].shape[0]

    def spec(at):
        return pl.BlockSpec((rows, block), lambda i: (at, i))

    in_specs = [pl.BlockSpec(x.shape, lambda i: (0, 0)) for x in left]
    in_specs += [spec(at) for _, at in flat]
    args = [*left, *[x for x, _ in flat]]
    if before is not None:
        in_specs.append(pl.BlockSpec((hidden, block), lambda i: (0, i)))
        args.append(before)
    if kind == "sum":
        out_shape = [jax.ShapeDtypeStruct((hidden, features), F32)]
        out_specs = [pl.BlockSpec((hidden, block), lambda i: (0, i))]
    elif kind == "blocks":
        width = features // N_DEPTH
        out_shape = [jax.ShapeDtypeStruct((N_DEPTH, own, width), BF16)]
        out_specs = [pl.BlockSpec((block // width, own, width), lambda i: (i, 0, 0))]
    else:
        out_shape = [jax.ShapeDtypeStruct((own, features), BF16)] * 2
        out_specs = [pl.BlockSpec((own, block), lambda i: (0, i))] * 2
    return pl.pallas_call(
        lambda *refs: weight_grad_kernel(n_groups, n_parts, before is not None, own, kind, *refs),
        grid=(features // block,),
        in_specs=in_specs,
        out_specs=out_specs,
        out_shape=out_shape,
        cost_estimate=cost(1),
        compiler_params=pltpu.CompilerParams(vmem_limit_bytes=40 * MIB),
    )(*args)


def transposed_kernel(left_ref, weight_ref, out_ref):
    out_ref[...] = times_transpose(left_ref[...], weight_ref[...]).astype(BF16)


def transposed_product(left, weight, block=896):
    width, features = weight.shape
    tokens = left.shape[0]
    return pl.pallas_call(
        transposed_kernel,
        grid=(width // block,),
        in_specs=[whole(left), pl.BlockSpec((block, features), lambda i: (i, 0))],
        out_specs=pl.BlockSpec((tokens, block), lambda i: (0, i)),
        out_shape=jax.ShapeDtypeStruct((tokens, width), BF16),
        cost_estimate=pl.CostEstimate(
            flops=8 * tokens * width * features,
            bytes_accessed=8 * width * features,
            transcendentals=0,
        ),
        compiler_params=pltpu.CompilerParams(vmem_limit_bytes=24 * MIB),
    )(left, weight)


def sums_at(refs, columns):
    return [
        mine[:, columns].astype(F32) + theirs[:, columns].astype(F32)
        for mine, theirs in zip(refs[::2], refs[1::2])
    ]


def mixed_kernel(*refs):
    weight_ref, out_ref, hidden_ref = refs[4:]

    @pl.when(pl.program_id(0) == 0)
    def _():
        for at in range(0, hidden_ref.shape[1], 512):
            columns = slice(at, at + 512)
            gate, up = sums_at(refs[:4], columns)
            hidden_ref[:, columns] = (gate * jax.nn.sigmoid(gate) * up).astype(BF16)

    out_ref[...] = plain(hidden_ref[...], weight_ref[...]).astype(BF16)


def whole(array):
    return pl.BlockSpec(array.shape, lambda i: (0, 0))


def mixed_product(gate_up, weight, block=512):
    width, features = weight.shape
    tokens = gate_up[0].shape[0]
    return pl.pallas_call(
        mixed_kernel,
        grid=(features // block,),
        in_specs=[*map(whole, gate_up), pl.BlockSpec((width, block), lambda i: (0, i))],
        out_specs=pl.BlockSpec((tokens, block), lambda i: (0, i)),
        out_shape=jax.ShapeDtypeStruct((tokens, features), BF16),
        scratch_shapes=[pltpu.VMEM((tokens, width), BF16)],
        cost_estimate=cost(1),
        compiler_params=pltpu.CompilerParams(vmem_limit_bytes=52 * MIB),
    )(*gate_up, weight)


def slice_grads_kernel(*refs):
    refs[6][...], refs[7][...] = gate_up_grads(*sums_at(refs[:6], slice(None)))


def slice_grads(values, block=512):
    tokens, width = values[0].shape
    spec = pl.BlockSpec((tokens, block), lambda i: (0, i))
    return pl.pallas_call(
        slice_grads_kernel,
        grid=(width // block,),
        in_specs=[spec] * 6,
        out_specs=[spec] * 2,
        out_shape=[jax.ShapeDtypeStruct((tokens, width), BF16)] * 2,
        cost_estimate=cost(1),
        compiler_params=pltpu.CompilerParams(vmem_limit_bytes=32 * MIB),
    )(*values)


def input_kernel(grad_gate_ref, grad_up_ref, gate_ref, up_ref, out_ref):
    total = times_transpose(grad_gate_ref[...], gate_ref[...])
    total += times_transpose(grad_up_ref[...], up_ref[...])
    out_ref[...] = total.astype(BF16)


def input_product(grads, gate_weight, up_weight, block=256):
    features, width = gate_weight.shape
    tokens = grads[0].shape[0]
    rows = pl.BlockSpec((block, width), lambda i: (i, 0))
    return pl.pallas_call(
        input_kernel,
        grid=(features // block,),
        in_specs=[*map(whole, grads), rows, rows],
        out_specs=pl.BlockSpec((tokens, block), lambda i: (0, i)),
        out_shape=jax.ShapeDtypeStruct((tokens, features), BF16),
        cost_estimate=cost(1),
        compiler_params=pltpu.CompilerParams(vmem_limit_bytes=52 * MIB),
    )(*grads, gate_weight, up_weight)


def added(terms, start, count):
    total = terms[0][start : start + count].astype(F32)
    for term in terms[1:]:
        total = total + term[start : start + count].astype(F32)
    return total.astype(BF16)


def per_device(tokens, gate_weight, up_weight, down_weight, cotangent):
    core = lax.axis_index("row").astype(jnp.int32).reshape(1)
    depth = lax.axis_index("depth")
    rows = tokens.shape[0]
    hidden_width = gate_weight.shape[1]
    own = hidden_width // N_DEPTH
    wide = -(-own // 128) * 128

    n = rows // 3
    thirds = [[(0, p * n, n), (1, p * n, n)] for p in range(3)]
    mine, zs, ys = regroup(
        core, [tokens, cotangent], [thirds[0] + thirds[1] + thirds[2], thirds[1], thirds[2]]
    )
    xs = [mine] + [shift(mine, "x", s) for s in (1, 2, -1)]
    zs, ys = ring(zs, "z"), ring(ys, "y")

    def joined(pieces, half):
        orders = ((0, 1, 2, 3), (0, 3, 2, 1))
        plans = [[[(i, c * half, half) for c in range(2) for i in order]] for order in orders]
        return regroup(core, pieces, *plans)[0]

    def stacked(pieces, half):
        return regroup(core, pieces, [[(i, c * half, half) for c in range(2) for i in range(4)]])[0]

    panel_plan = [[(i, 2 * n * p + n * c, n) for i in range(4) for p in range(3)] for c in range(2)]
    first_plan = [(i, n * c, n) for c in range(2) for i in range(4)]
    panel, grad_panel, r0 = regroup(core, xs, [*panel_plan, first_plan])
    t0, q0 = joined(zs, n), joined(ys, n)
    r1, t1, q1 = hop(r0, "y"), hop(t0, "x"), hop(q0, "z")

    def own_columns(weight):
        cut = lax.dynamic_slice_in_dim(weight, depth * own, own, axis=1)
        return jnp.pad(cut, ((0, 0), (0, wide - own)))

    own_gate_up = jnp.concatenate([own_columns(gate_weight), own_columns(up_weight)], axis=1)
    own_down = jnp.pad(
        lax.dynamic_slice_in_dim(down_weight, depth * own, own, axis=0), ((0, wide - own), (0, 0))
    )

    (panel_,) = tie((panel,), r0, own_gate_up, own_down)
    gate_part = plain(panel_, gate_weight).astype(BF16)

    (panel_,) = tie((panel,), gate_part, r1, t1, q1)
    (r1_, t1_, q1_) = tie((r1, t1, q1), gate_part)
    r2, t2, q2 = hop(r1_, "y"), hop(t1_, "x"), hop(q1_, "z")
    up_part = plain(panel_, up_weight).astype(BF16)
    gate_theirs = swap(gate_part)

    (grad_panel,) = tie((grad_panel,), up_part, r2, t2, q2, gate_theirs)
    (r2_, t2_, q2_) = tie((r2, t2, q2), up_part)
    r3, t3, q3 = hop(r2_, "y"), hop(t2_, "x"), hop(q2_, "z")
    up_theirs = swap(up_part)
    grad_part = transposed_product(grad_panel, down_weight)

    r0, r1, r2, r3 = tie((r0, r1, r2, r3), grad_part, up_theirs)
    t0, t1, t2, t3 = tie((t0, t1, t2, t3), grad_part)
    q0, q1, q2, q3 = tie((q0, q1, q2, q3), grad_part)
    grad_theirs = swap(grad_part)
    axes = ("z", "y", "x")

    def hops(pieces, *deps):
        return [hop(*tie((x,), *deps), axis) for x, axis in zip(pieces, axes)]

    both = [[stacked(x, 4 * n) for x in ((r0, r1, r2, r3), (t0, t1, t2, t3), (q0, q1, q2, q3))]]
    both.append(hops(both[0]))
    toks, cots = [[(x, 0) for x in both[0]]], [[(x, 1) for x in both[0]]]
    (gate_part_,) = tie((gate_part,), *both[0])
    gate_up = (gate_theirs, up_part, up_theirs)
    mixed_part = mixed_product((gate_part_, *gate_up), down_weight)
    (own_down_,) = tie((own_down,), mixed_part)
    u0 = own_partials([toks[0], cots[0]], (own_gate_up, own_down_), (0, 1))
    v0 = swap(u0)
    (gate_part_,) = tie((gate_part,), u0)
    grads = slice_grads((gate_part_, *gate_up, grad_part, grad_theirs))

    both.append(hops(both[1], *grads, v0))
    toks.append([(x, 0) for x in both[1]])
    cots.append([(x, 1) for x in both[1]])
    input_part = input_product(tie(tuple(grads), *both[1]), gate_weight, up_weight)
    (own_down_,) = tie((own_down,), input_part)
    u1 = own_partials([toks[1], cots[1]], (own_gate_up, own_down_), (0, 1))
    v1 = swap(u1)
    back_plan = [[(p, back * rows, rows) for p in range(2)] for back in range(N_COL)]
    sums = regroup(core, [mixed_part, input_part], back_plan)

    both.append(hops(both[2], u1, v0, v1, *sums))
    toks.append([(x, 0) for x in both[2]])
    cots.append([(x, 1) for x in both[2]])
    (own_down_,) = tie((own_down,), u1, *both[2])
    u2 = own_partials([toks[2], cots[2]], (own_gate_up, own_down_), (0, 1))
    v2 = swap(u2)

    def hidden_of(mine, theirs):
        return activations(hidden_kernel, wide, *[(x, 2 * wide, 0) for x in (mine, theirs)])

    def grads_of(mine, theirs, *grads):
        pre = [(x, 2 * wide, 0) for x in (mine, theirs)]
        return activations(grads_kernel, 2 * wide, *pre, *[(x, wide, at) for x, at in grads])

    (u0,) = tie((u0,), u2)
    h0 = hidden_of(u0, v0)
    d0 = grads_of(u0, v0, (u0, 2), (v0, 2))
    (u2,) = tie((u2,), d0)
    h2 = hidden_of(u2, v2)
    d2 = grads_of(u2, v2, (u2, 2), (v2, 2))
    (h2,) = tie((h2,), d2)
    (down_early,) = weight_grad([h0, h2], [cots[0], cots[2]], "sum", own)
    (d2,) = tie((d2,), down_early)
    (grads_early,) = weight_grad([d0, d2], [toks[0], toks[2]], "sum", own)

    toks.append([(x, 0) for x in both[3]])
    cots.append([(x, 1) for x in both[3]])
    (own_gate_up_,) = tie((own_gate_up,), grads_early, *both[3])
    u3 = own_partials([toks[3]], (own_gate_up_, None), (0,))
    v3 = swap(u3)
    h3 = hidden_of(u3, v1)
    (u1,) = tie((u1,), h3)
    h1 = hidden_of(u1, v3)
    (down_blocks,) = weight_grad([h1, h3], [cots[1], cots[3]], "blocks", own, before=down_early)
    down_grad = lax.all_to_all(down_blocks, "depth", split_axis=0, concat_axis=0, tiled=True)

    (own_down_,) = tie((own_down,), h3)
    w3 = own_partials([cots[3]], (None, own_down_), (1,))
    z3 = swap(w3)
    (u3,) = tie((u3,), down_blocks)
    d3 = grads_of(u3, v1, (w3, 0), (v1, 2))
    sums = tie(tuple(sums), u3)
    sums = [sums[0]] + [shift(sums[back], "x", -back) for back in range(1, N_COL)]
    d1 = grads_of(u1, v3, (u1, 2), (z3, 0))
    gate_grad, up_grad = weight_grad(
        [d1, d3], [toks[1], toks[3]], "pair", own, before=grads_early
    )
    down_grad = down_grad.reshape(hidden_width, -1)
    sums = tie(tuple(sums), gate_grad)
    mixed, input_grad = added(sums, 0, rows), added(sums, rows, rows)
    return mixed, input_grad, gate_grad.T, up_grad.T, down_grad


def solution(mesh):
    placed = (
        P(("col", "depth"), "row"),
        P("row", "col"),
        P("row", "col"),
        P("col", "row"),
        P(("col", "depth"), "row"),
    )
    return jax.shard_map(
        per_device,
        mesh=mesh,
        in_specs=placed,
        out_specs=(
            P(("col", "depth"), "row"),
            P(("col", "depth"), "row"),
            P("row", ("col", "depth")),
            P("row", ("col", "depth")),
            P("col", ("row", "depth")),
        ),
        check_vma=False,
    )
```
